1024 devices in a mesh: dp: 32 (over z_hi, y, core), seq: 32 (over z_lo, x).
Axes of the slice: x: 8, y: 8, z: 8 (z_hi: 2, z_lo: 4; z = z_hi * 4 + z_lo), core: 2. Of those that a mesh axis runs over, the one named last changes fastest.
Arguments:
- dna_bases: int32 [32, 32768], P('dp', 'seq'), may hold values from 0 to 4, as said below
- conv_weight: bfloat16 [5, 5, 1536], replicated, may hold values from -2.5 to 2.5
- conv_bias: float32 [1536], replicated, may hold values from -3 to 3
- w_query: bfloat16 [1536, 768], replicated, may hold values from -1 to 1
- w_key: bfloat16 [1536, 768], replicated, may hold values from -1 to 1
- w_value: bfloat16 [1536, 768], replicated, may hold values from -0.15625 to 0.15625
- out_grad: bfloat16 [32, 256, 768], P('dp', 'seq'), may hold values from -6 to 6
Outputs:
- attended: bfloat16 [32, 256, 768], P('dp', 'seq')
- pooled: bfloat16 [32, 256, 1536], P('dp', 'seq')
- conv_grad: float32 [5, 5, 1536], replicated
- bias_grad: float32 [1536], replicated
The draws below stay inside these ranges and needn't reach their ends.
Inputs may be any that keep to these rules, and one draw needn't show every extreme that they name: `dna_bases`: letter codes A, C, G, T, N.
All inputs are finite; a program needn't handle non-finite values.
Results may differ from the reference program's by a relative error of at most 0.0103.
Values may be sent and summed in bfloat16 or wider, within the bound.
A program may use at most 32 MiB of HBM per device.

```python
import jax
import jax.numpy as jnp
from jax import lax

C = 1536
HEADS = 4
HEAD = 192
KERNEL = 5
LETTERS = 5
POOL = 128
INNER = 768
GENOMES = 32
LENGTH = 32768
ROWS = 256


def draw_dna_bases(key, part):
    key = jax.random.fold_in(key, 5)
    keys_four = jax.random.split(key, 4)
    block_count = LENGTH // POOL
    favoured = jax.random.randint(keys_four[0], (GENOMES, block_count, 1), 0, 5)
    level = jax.random.randint(keys_four[1], (GENOMES, block_count, 1), 0, 8)
    picked = jax.random.randint(keys_four[2], (GENOMES, block_count, POOL), 0, 8)
    others = jax.random.randint(keys_four[3], (GENOMES, block_count, POOL), 0, 5)
    letters_drawn = jnp.where(picked < level, favoured, others)
    return letters_drawn.reshape(GENOMES, LENGTH).astype(jnp.int32)


def draw_w_query(key, part):
    key = jax.random.fold_in(key, 21)
    own_part = jnp.clip(jax.random.normal(key, (C, INNER), jnp.float32), -4.0, 4.0)
    mixed = own_part
    return jnp.clip(mixed * C ** (-0.5), -1.0, 1.0).astype(jnp.bfloat16)


def draw_w_key(key, part):
    key = jax.random.fold_in(key, 37)
    own_part = jnp.clip(jax.random.normal(key, (C, INNER), jnp.float32), -4.0, 4.0)
    mixed = own_part
    return jnp.clip(mixed * C ** (-0.5), -1.0, 1.0).astype(jnp.bfloat16)


def steps_of(own_key, dims, cuts, low, top_value):
    level, own = 1.0, jax.random.fold_in(own_key, 6)
    for axis_at, shards_of in cuts:
        heights = jnp.exp(jax.random.uniform(jax.random.fold_in(own, axis_at), (shards_of,), jnp.float32, low / len(cuts), top_value / len(cuts)))
        level = level * jnp.repeat(heights, dims[axis_at] // shards_of).reshape([-1 if axis == axis_at else 1 for axis in range(len(dims))])
    return level


def centred(own_key, dims, deviation, reach, shards=(), kind=jnp.bfloat16):
    entries = jax.random.normal(own_key, dims, jnp.float32) * deviation
    if len(shards) > 0:
        entries = steps_of(own_key, dims, shards, -0.22, 0.18) * entries
    return jnp.clip(entries, min=-reach, max=reach).astype(kind)


def setup_inputs(seed: int = 0) -> dict:
    key_of = jax.random.split(jax.random.key(seed), 8)
    dna_bases = draw_dna_bases(jax.random.fold_in(key_of[7], 71), 0)
    conv_weight = centred(key_of[1], (KERNEL, LETTERS, C), KERNEL ** -0.5, 2.5)
    conv_bias = centred(key_of[2], (C,), 0.5, 3.0, (), jnp.float32)
    w_query = draw_w_query(jax.random.fold_in(key_of[7], 71), 0)
    w_key = draw_w_key(jax.random.fold_in(key_of[7], 71), 0)
    w_value = centred(key_of[5], (C, INNER), C ** -0.5, 0.15625)
    out_grad = centred(key_of[6], (GENOMES, ROWS, INNER), 1.0, 6.0, ((0, 32), (1, 32)))
    return dict(dna_bases=dna_bases, conv_weight=conv_weight, conv_bias=conv_bias, w_query=w_query, w_key=w_key, w_value=w_value, out_grad=out_grad)


def tap_letters(window, tap_count):
    tap_codes = jnp.stack([window[offset:offset + tap_count] for offset in range(KERNEL)], axis=1)
    letter_codes = jnp.arange(1, LETTERS + 1, dtype=jnp.int32)
    return (tap_codes[:, :, None] == letter_codes[None, None, :]).reshape(tap_count, KERNEL * LETTERS)

def conv_pre(one_hot, conv_weight, conv_bias):
    tap_table = conv_weight.reshape(KERNEL * LETTERS, C)
    return jnp.dot(one_hot.astype(jnp.bfloat16), tap_table, preferred_element_type=jnp.float32) + conv_bias

def pooled_rows(extended, conv_weight, conv_bias):
    tap_count = 4 * POOL
    block_count = (extended.shape[1] - 4) // tap_count

    def one_genome(row_codes):

        def one_block(block_index):
            window = lax.dynamic_slice_in_dim(row_codes, block_index * tap_count, tap_count + 4)
            activated = jax.nn.gelu(conv_pre(tap_letters(window, tap_count), conv_weight, conv_bias))
            return activated.reshape(4, POOL, C).mean(axis=1).astype(jnp.bfloat16)
        blocks_out = lax.map(one_block, jnp.arange(block_count, dtype=jnp.int32))
        return blocks_out.reshape(block_count * 4, C)
    return lax.map(one_genome, extended)

def conv_grads(extended, d_pooled, conv_weight, conv_bias):
    tap_count = 4 * POOL
    block_count = (extended.shape[1] - 4) // tap_count
    start_sums = (jnp.zeros((KERNEL * LETTERS, C), jnp.float32), jnp.zeros((C,), jnp.float32))

    def one_genome(totals, pair):
        row_codes, d_rows = pair

        def one_block(sums, block_index):
            window = lax.dynamic_slice_in_dim(row_codes, block_index * tap_count, tap_count + 4)
            one_hot = tap_letters(window, tap_count)
            pre_act = conv_pre(one_hot, conv_weight, conv_bias)
            d_block = lax.dynamic_slice_in_dim(d_rows, block_index * 4, 4, 0)
            d_act = jnp.repeat(d_block, POOL, axis=0) * (1.0 / POOL)
            d_pre = jax.vjp(jax.nn.gelu, pre_act)[1](d_act)[0]
            weight_sum = sums[0] + jnp.einsum('pk,pc->kc', one_hot.astype(jnp.float32), d_pre, precision=lax.Precision.HIGHEST)
            return ((weight_sum, sums[1] + lax.optimization_barrier(jnp.sum(d_pre, axis=0))), None)
        totals, _ = lax.scan(one_block, totals, jnp.arange(block_count, dtype=jnp.int32))
        return (totals, None)
    totals, _ = lax.scan(one_genome, start_sums, (extended, d_pooled))
    return totals

def attention_side(query_rows, grad_rows, key_rows, value_rows):
    heads_q = query_rows.reshape(-1, HEADS, HEAD).astype(jnp.float32)
    heads_k = key_rows.reshape(-1, HEADS, HEAD).astype(jnp.float32)
    heads_v = value_rows.reshape(-1, HEADS, HEAD).astype(jnp.float32)
    heads_g = grad_rows.reshape(-1, HEADS, HEAD).astype(jnp.float32)
    scores = jnp.einsum('qhd,khd->hqk', heads_q, heads_k) * HEAD ** (-0.5)
    row_max = lax.optimization_barrier(jnp.max(scores, axis=-1, keepdims=True))
    weights = jnp.exp(scores - row_max)
    soft_out = weights / lax.optimization_barrier(jnp.sum(weights, axis=-1, keepdims=True))
    soft_half = lax.optimization_barrier(soft_out.astype(jnp.bfloat16)).astype(jnp.float32)
    attended = jnp.einsum('hqk,khd->qhd', soft_half, heads_v).reshape(-1, INNER).astype(jnp.bfloat16)
    d_value = jnp.einsum('hqk,qhd->khd', soft_half, heads_g).reshape(-1, INNER)
    d_soft = jnp.einsum('qhd,khd->hqk', heads_g, heads_v)
    row_delta = lax.optimization_barrier(jnp.sum(soft_out * d_soft, axis=-1, keepdims=True))
    d_scores = soft_out * (d_soft - row_delta) * HEAD ** (-0.5)
    d_half = lax.optimization_barrier(d_scores.astype(jnp.bfloat16)).astype(jnp.float32)
    d_query = jnp.einsum('hqk,khd->qhd', d_half, heads_k).reshape(-1, INNER).astype(jnp.bfloat16)
    d_key = jnp.einsum('hqk,qhd->khd', d_half, heads_q).reshape(-1, INNER)
    return (attended, d_query, d_key.astype(jnp.bfloat16), d_value.astype(jnp.bfloat16))

def reference(dna_bases, conv_weight, conv_bias, w_query, w_key, w_value, out_grad):
    extended = jnp.pad(dna_bases + 1, ((0, 0), (2, 2)))
    pooled = pooled_rows(extended, conv_weight, conv_bias)
    flat = pooled.reshape(-1, C)
    query_rows = jnp.dot(flat, w_query, preferred_element_type=jnp.float32).astype(jnp.bfloat16).reshape(GENOMES, ROWS, INNER)
    key_rows = jnp.dot(flat, w_key, preferred_element_type=jnp.float32).astype(jnp.bfloat16).reshape(GENOMES, ROWS, INNER)
    value_rows = jnp.dot(flat, w_value, preferred_element_type=jnp.float32).astype(jnp.bfloat16).reshape(GENOMES, ROWS, INNER)
    attended, d_query, d_key, d_value = lax.map(lambda parts: attention_side(*parts), (query_rows, out_grad, key_rows, value_rows))
    d_pooled = jnp.dot(d_query.reshape(-1, INNER), w_query.T, preferred_element_type=jnp.float32)
    d_pooled = d_pooled + jnp.dot(d_key.reshape(-1, INNER), w_key.T, preferred_element_type=jnp.float32)
    d_pooled = d_pooled + jnp.dot(d_value.reshape(-1, INNER), w_value.T, preferred_element_type=jnp.float32)
    conv_grad, bias_grad = conv_grads(extended, d_pooled.reshape(GENOMES, ROWS, C), conv_weight, conv_bias)
    return (attended, pooled, conv_grad.reshape(KERNEL, LETTERS, C), bias_grad)
```

```python
import functools

import jax
import jax.numpy as jnp
from jax import lax
from jax.experimental import pallas as pl
from jax.experimental.pallas import tpu as pltpu
from jax.sharding import PartitionSpec as P

C = 1536
HEAD = 192
LETTERS = 5
POOL = 128
INNER = 768
ROWS = 8
SPAN = ROWS * POOL
CODES = 48
WIDE = 256
LANES = 256
DEPTH = 4
RING = 8
SEQ = DEPTH * RING
CHIPS = 16
GELU_A = 0.7978845608028654
GELU_B = 0.044715
NT = (((1,), (1,)), ((), ()))
MESH = pl.DeviceIdType.MESH
F32 = jnp.float32
BF16 = jnp.bfloat16


def window_start(head):
    return 384 * (head // 2) + 128 * (head % 2)


def one_hot_rows(codes):
    width = codes.shape[1]
    wide = jnp.broadcast_to(codes, (8, width))
    letter = lax.broadcasted_iota(jnp.int32, (8, width - 256), 0)
    parts = []
    for tap in range(5):
        moved = wide if tap == 2 else pltpu.roll(wide, (2 - tap) % width, 1)
        hit = moved[:, 128 : width - 128] == letter
        if tap == 0:
            hit = jnp.logical_or(hit, letter >= LETTERS)
        parts.append(jnp.where(hit, 1.0, 0.0).astype(F32))
    parts.append(jnp.zeros_like(parts[0]))
    return jnp.concatenate(parts, axis=0)


def positions_first(rows):
    full = jnp.concatenate([rows, jnp.zeros((128 - CODES, rows.shape[1]), F32)], axis=0)
    blocks = [full[:, at : at + 128].T for at in range(0, rows.shape[1], 128)]
    return jnp.concatenate(blocks, axis=0)


def gelu_twice(x):
    square = x * x
    inner = x * (square * (GELU_A * GELU_B) + GELU_A)
    tanh = jnp.tanh(inner)
    return x + x * tanh, square, tanh


def gelu_slope_twice(x, square, tanh):
    return (1.0 + tanh) + (x - x * (tanh * tanh)) * (square * (3 * GELU_A * GELU_B) + GELU_A)


def stem_kernel(
    dna_hbm, taps_hbm, bias_hbm, wq_hbm, wk_hbm, wv_hbm, grad_hbm,
    attended_ref, pooled_ref, conv_ref, conv_bias_ref,
    dna_ref, taps_ref, bias_ref, grad_ref, weights, table, hot, hot_t, pooled_sum, slopes, halo,
    grad_send, grad_rows, grad_all, pool_rows, qkv_all, back_send, back_rows,
    acc, core_part, tiles, scatter_rows, chip_rows, full,
    load_sem, halo_ss, halo_rs, g1_ss, g1_rs, g2_ss, g2_rs, p_ss, p_rs, q_ss, q_rs, b_ss, b_rs,
    c_ss, c_rs, s_ss, s_rs,
):
    dp = lax.axis_index("dp")
    seq = lax.axis_index("seq")
    head = lax.div(seq, RING)
    col = lax.rem(seq, RING)
    chip = lax.div(dp, 2)
    core = lax.rem(dp, 2)

    def in_seq(index):
        return (dp, index)

    def along_z(step):
        return in_seq(lax.rem(head + (step + DEPTH), DEPTH) * RING + col)

    def along_x(step):
        return in_seq(head * RING + lax.rem(col + step, RING))

    def along_seq(step):
        return in_seq(lax.rem(seq + (step + SEQ), SEQ))

    def along_chips(step):
        return (lax.rem(chip + step, CHIPS) * 2 + core, seq)

    other_core = (chip * 2 + (1 - core), seq)

    def remote(src, dst, ss, rs, device):
        return pltpu.make_async_remote_copy(
            src_ref=src, dst_ref=dst, send_sem=ss, recv_sem=rs, device_id=device, device_id_type=MESH
        )

    small = ((dna_hbm, dna_ref), (taps_hbm, taps_ref), (bias_hbm, bias_ref), (grad_hbm, grad_ref))
    reads = [pltpu.make_async_copy(hbm, ref, load_sem.at[3 + i]) for i, (hbm, ref) in enumerate(small)]
    loads = [
        pltpu.make_async_copy(hbm, weights.at[i], load_sem.at[i])
        for i, hbm in enumerate((wq_hbm, wk_hbm, wv_hbm))
    ]
    for copy in (*reads, *loads):
        copy.start()

    barrier = pltpu.get_barrier_semaphore()

    def greet(device):
        pl.semaphore_signal(barrier, inc=1, device_id=device, device_id_type=MESH)

    def greet_seq(step, _):
        greet(along_seq(step))
        return 0

    def greet_chips(step, _):
        greet(along_chips(step))
        return 0

    lax.fori_loop(1, SEQ, greet_seq, 0)
    lax.fori_loop(1, CHIPS, greet_chips, 0)
    greet(other_core)


    for copy in reads:
        copy.wait()

    bias = bias_ref[...].reshape(1, C)
    bias_high = bias.astype(BF16).astype(F32)
    bias_mid = (bias - bias_high).astype(BF16).astype(F32)
    bias_low = bias - bias_high - bias_mid
    for tap in range(5):
        letters = taps_ref[tap].astype(F32)
        spare = [bias_high, bias_mid, bias_low] if tap == 0 else [jnp.zeros((3, C), F32)]
        pair = jnp.concatenate([letters, *spare], axis=0)
        acc[8 * tap : 8 * tap + 8, :] = pair
    table[0:48, :] = jnp.concatenate([acc[...], jnp.zeros((8, C), F32)], axis=0).astype(BF16)
    table[48:128, :] = jnp.zeros((80, C), BF16)

    codes = dna_ref[...]
    outside = jnp.full((1, 128), -1, jnp.int32)
    rows = one_hot_rows(jnp.concatenate([outside, codes, outside], axis=1))
    hot_t[...] = rows.astype(BF16)
    hot[...] = positions_first(rows).astype(BF16)

    def pre_act(block, lanes):
        return jnp.dot(
            hot[block * POOL : (block + 1) * POOL, :], table[:, lanes], preferred_element_type=F32
        )

    def slope_sums(block, lanes, slope):
        slopes[block, :, lanes] = jnp.dot(
            hot_t[:, block * POOL : (block + 1) * POOL],
            slope.astype(BF16),
            preferred_element_type=F32,
        )

    def lanes_of(part):
        return pl.ds(pl.multiple_of(part * LANES, LANES), LANES)

    def inner_blocks(part, _):
        lanes = lanes_of(part)
        for block in range(1, ROWS - 1):
            x = pre_act(block, lanes)
            twice, square, tanh = gelu_twice(x)
            pooled_sum[block : block + 1, lanes] = jnp.sum(twice, axis=0, keepdims=True)
            slope_sums(block, lanes, gelu_slope_twice(x, square, tanh))
        return 0

    def end_pools(part, _):
        lanes = lanes_of(part)
        for block in (0, ROWS - 1):
            twice, _, _ = gelu_twice(pre_act(block, lanes))
            pooled_sum[block : block + 1, lanes] = jnp.sum(twice, axis=0, keepdims=True)
        return 0

    def end_slopes(part, _):
        lanes = lanes_of(part)
        for block in (0, ROWS - 1):
            x = pre_act(block, lanes)
            _, square, tanh = gelu_twice(x)
            slope_sums(block, lanes, gelu_slope_twice(x, square, tanh))
        return 0

    lane = lax.broadcasted_iota(jnp.int32, (ROWS, WIDE), 1)
    grad = grad_ref[0].astype(F32)
    for h in range(DEPTH):
        low = 64 * (h % 2)
        start = window_start(h)
        keep = jnp.logical_and(lane >= low, lane < low + HEAD)
        window = jnp.where(keep, grad[:, start : start + WIDE], 0.0)
        grad_send[h] = jnp.concatenate([window[:, :128], window[:, 128:]], axis=0).astype(BF16)

    lax.fori_loop(0, C // LANES // 2, inner_blocks, 0)
    pl.semaphore_wait(barrier, SEQ - 1 + CHIPS - 1 + 1)

    halo_sends = [
        remote(dna_ref.at[:, SPAN - 128 : SPAN], halo.at[0], halo_ss.at[0], halo_rs.at[0], along_seq(1)),
        remote(dna_ref.at[:, 0:128], halo.at[1], halo_ss.at[1], halo_rs.at[1], along_seq(-1)),
    ]
    for copy in halo_sends:
        copy.start()
    g1 = [
        remote(
            grad_send.at[lax.rem(head + step, DEPTH)], grad_rows.at[step],
            g1_ss.at[step], g1_rs.at[step], along_z(step),
        )
        for step in range(1, DEPTH)
    ]
    for copy in g1:
        copy.start()
    grad_rows[0] = grad_send[head]

    lax.fori_loop(C // LANES // 2, C // LANES, inner_blocks, 0)

    for copy in halo_sends:
        copy.wait()
    before = jnp.where(seq == 0, -1, halo[0])
    after = jnp.where(seq == SEQ - 1, -1, halo[1])
    first = one_hot_rows(jnp.concatenate([before, codes[:, :256]], axis=1))
    last = one_hot_rows(jnp.concatenate([codes[:, SPAN - 256 :], after], axis=1))
    hot_t[:, :POOL] = first.astype(BF16)
    hot_t[:, SPAN - POOL :] = last.astype(BF16)
    hot[:POOL, :] = positions_first(first).astype(BF16)
    hot[SPAN - POOL :, :] = positions_first(last).astype(BF16)
    lax.fori_loop(0, C // LANES, end_pools, 0)

    pooled = pooled_sum[...] * (0.5 / POOL)
    pooled_ref[0] = pooled.astype(BF16)
    pool_rows[0] = jnp.concatenate([pooled[:, :INNER], pooled[:, INNER:]], axis=0).astype(BF16)
    p1 = [
        remote(pool_rows.at[0], pool_rows.at[step], p_ss.at[step], p_rs.at[step], along_z(step))
        for step in range(1, DEPTH)
    ]
    for copy in p1:
        copy.start()

    for copy in g1:
        copy.wait()
    blocks = grad_rows[...].astype(F32)
    grad_all[0] = jnp.concatenate(
        [jnp.concatenate([blocks[i, :8], blocks[i, 8:]], axis=1) for i in range(DEPTH)], axis=0
    ).astype(BF16)
    g2 = [
        remote(grad_all.at[0], grad_all.at[step], g2_ss.at[step], g2_rs.at[step], along_x(step))
        for step in range(1, RING)
    ]
    for copy in g2:
        copy.start()

    lax.fori_loop(0, C // LANES, end_slopes, 0)

    for load in loads:
        load.wait()
    for copy in p1:
        copy.wait()
    start = pl.multiple_of(384 * lax.div(head, 2) + 128 * lax.rem(head, 2), 128)
    low = 64 * lax.rem(head, 2)
    lane = lax.broadcasted_iota(jnp.int32, (4 * ROWS, WIDE), 1)
    keep = jnp.logical_and(lane >= low, lane < low + HEAD)
    halves = pool_rows[...].reshape(DEPTH * 16, INNER)
    for i in range(3):
        left = jnp.dot(halves, weights[i, :INNER, pl.ds(start, WIDE)], preferred_element_type=F32)
        right = jnp.dot(halves, weights[i, INNER:, pl.ds(start, WIDE)], preferred_element_type=F32)
        rows = jnp.concatenate(
            [left[16 * j : 16 * j + 8] + right[16 * j + 8 : 16 * j + 16] for j in range(DEPTH)], axis=0
        )
        qkv_all[0, 32 * i : 32 * i + 32, :] = jnp.where(keep, rows, 0.0).astype(BF16)
    q1 = [
        remote(qkv_all.at[0], qkv_all.at[step], q_ss.at[step], q_rs.at[step], along_x(step))
        for step in range(1, RING)
    ]
    for copy in q1:
        copy.start()
    for copy in g2:
        copy.wait()
    for copy in q1:
        copy.wait()

    everyone = RING * 32
    q = qkv_all[:, 0:32, :].reshape(everyone, WIDE)
    k = qkv_all[:, 32:64, :].reshape(everyone, WIDE)
    v = qkv_all[:, 64:96, :].reshape(everyone, WIDE)
    g = grad_all[...].reshape(everyone, WIDE)
    scale = HEAD ** (-0.5)

    def soft_parts(scores, d_soft, axis):
        scores = scores * scale
        shifted = jnp.exp(scores - jnp.max(scores, axis=axis, keepdims=True))
        soft = shifted / jnp.sum(shifted, axis=axis, keepdims=True)
        delta = jnp.sum(soft * d_soft, axis=axis, keepdims=True)
        return soft, delta

    def finish(soft, d_soft, delta):
        return soft.astype(BF16), (soft * (d_soft - delta) * scale).astype(BF16)

    scores_t = lax.dot_general(k, q, NT, preferred_element_type=F32)
    d_soft_t = lax.dot_general(v, g, NT, preferred_element_type=F32)
    scores_own = lax.dot_general(q[:32], k, NT, preferred_element_type=F32)
    d_soft_own = lax.dot_general(g[:32], v, NT, preferred_element_type=F32)
    soft_t, delta_t = soft_parts(scores_t, d_soft_t, 0)
    half_t, d_half_t = finish(soft_t[:32], d_soft_t[:32], delta_t)
    soft_own, delta_own = soft_parts(scores_own, d_soft_own, 1)
    half_own, d_half_own = finish(soft_own, d_soft_own, delta_own)
    results = (
        jnp.dot(half_own, v, preferred_element_type=F32),
        jnp.dot(d_half_own, k, preferred_element_type=F32),
        jnp.dot(d_half_t, q, preferred_element_type=F32),
        jnp.dot(half_t, g, preferred_element_type=F32),
    )
    for i in range(DEPTH):
        mine = jnp.concatenate([result[8 * i : 8 * i + 8] for result in results], axis=0).astype(BF16)
        if i == 0:
            back_rows[0] = mine
        else:
            back_send[i] = mine
    b1 = [
        remote(back_send.at[i], back_rows.at[i], b_ss.at[i], b_rs.at[i], along_z(-i))
        for i in range(1, DEPTH)
    ]
    for copy in b1:
        copy.start()
    for copy in b1:
        copy.wait()

    by_head = [back_rows[lax.rem(h - head + DEPTH, DEPTH)].astype(F32) for h in range(DEPTH)]

    def joined(i):
        a, b, c, d = (rows[8 * i : 8 * i + 8] for rows in by_head)
        return jnp.concatenate(
            [a[:, :128], a[:, 128:] + b[:, :128], b[:, 128:], c[:, :128], c[:, 128:] + d[:, :128], d[:, 128:]],
            axis=1,
        ).astype(BF16)

    attended_ref[0] = joined(0)
    d_pooled = lax.dot_general(joined(1), weights[0], NT, preferred_element_type=F32)
    d_pooled += lax.dot_general(joined(2), weights[1], NT, preferred_element_type=F32)
    d_pooled += lax.dot_general(joined(3), weights[2], NT, preferred_element_type=F32)
    d_pooled *= 0.5 / POOL
    total = slopes[0, 0:40, :] * d_pooled[0:1]
    for block in range(1, ROWS):
        total += slopes[block, 0:40, :] * d_pooled[block : block + 1]
    acc[...] = total

    half = C // 2
    theirs = pl.ds(pl.multiple_of((1 - core) * half, 128), half)
    ours = pl.ds(pl.multiple_of(core * half, 128), half)
    swap = remote(acc.at[:, theirs], core_part, c_ss.at[0], c_rs.at[0], other_core)
    swap.start()
    swap.wait()
    both = acc[:, ours] + core_part[...]
    for tap in range(5):
        for part in range(6):
            tiles[6 * tap + part] = both[8 * tap : 8 * tap + 8, 128 * part : 128 * part + 128]
    tiles[30:32] = jnp.zeros((2, 8, 128), F32)

    def scatter(step, _):
        to = lax.rem(seq + step, SEQ)
        remote(tiles.at[to], scatter_rows.at[step], s_ss.at[0], s_rs.at[0], in_seq(to)).start()
        return 0

    def spread(step, _):
        remote(chip_rows.at[0], chip_rows.at[step], s_ss.at[1], s_rs.at[1], along_chips(step)).start()
        return 0

    def gather(step, _):
        mine = full.at[core, seq]
        remote(mine, mine, s_ss.at[2], s_rs.at[2], along_seq(step)).start()
        return 0

    lax.fori_loop(1, SEQ, scatter, 0)
    arrived = scatter_rows.at[1:SEQ]
    remote(arrived, arrived, s_ss.at[0], s_rs.at[0], other_core).wait()
    chip_rows[0] = tiles[seq] + jnp.sum(scatter_rows[1:SEQ], axis=0)
    lax.fori_loop(1, CHIPS, spread, 0)
    arrived = chip_rows.at[1:CHIPS]
    remote(arrived, arrived, s_ss.at[1], s_rs.at[1], other_core).wait()
    tile = chip_rows[chip]
    for i in range(1, CHIPS):
        tile += chip_rows[lax.rem(chip + (CHIPS - i), CHIPS)]
    full[core, seq] = tile
    lax.fori_loop(1, SEQ, gather, 0)
    arrived = full.at[core, 0 : SEQ - 1]
    remote(arrived, arrived, s_ss.at[2], s_rs.at[2], other_core).wait()
    swap = remote(full.at[core], full.at[core], c_ss.at[1], c_rs.at[1], other_core)
    swap.start()
    swap.wait()
    for side in range(2):
        for tap in range(5):
            for part in range(6):
                lanes = slice(half * side + 128 * part, half * side + 128 * part + 128)
                conv_ref[tap, :, lanes] = full[side, 6 * tap + part, 0:LETTERS, :]
                if tap == 0:
                    conv_bias_ref[lanes] = full[side, part, LETTERS, :]


def per_device(dna_bases, conv_weight, conv_bias, w_query, w_key, w_value, out_grad):
    vmem = pl.BlockSpec(memory_space=pltpu.VMEM)
    hbm = pl.BlockSpec(memory_space=pl.ANY)
    dma = pltpu.SemaphoreType.DMA
    return pl.pallas_call(
        stem_kernel,
        name="genomic_stem",
        out_shape=(
            jax.ShapeDtypeStruct((1, ROWS, INNER), BF16),
            jax.ShapeDtypeStruct((1, ROWS, C), BF16),
            jax.ShapeDtypeStruct((5, LETTERS, C), F32),
            jax.ShapeDtypeStruct((C,), F32),
        ),
        in_specs=[hbm] * 7,
        out_specs=(vmem, vmem, vmem, vmem),
        scratch_shapes=[
            pltpu.VMEM((1, SPAN), jnp.int32),
            pltpu.VMEM((5, LETTERS, C), BF16),
            pltpu.VMEM((C,), F32),
            pltpu.VMEM((1, ROWS, INNER), BF16),
            pltpu.VMEM((3, C, INNER), BF16),
            pltpu.VMEM((128, C), BF16),
            pltpu.VMEM((SPAN, 128), BF16),
            pltpu.VMEM((CODES, SPAN), BF16),
            pltpu.VMEM((ROWS, C), F32),
            pltpu.VMEM((ROWS, CODES, C), F32),
            pltpu.VMEM((2, 1, 128), jnp.int32),
            pltpu.VMEM((DEPTH, 16, 128), BF16),
            pltpu.VMEM((DEPTH, 16, 128), BF16),
            pltpu.VMEM((RING, 32, WIDE), BF16),
            pltpu.VMEM((DEPTH, 16, INNER), BF16),
            pltpu.VMEM((RING, 96, WIDE), BF16),
            pltpu.VMEM((DEPTH, 32, WIDE), BF16),
            pltpu.VMEM((DEPTH, 32, WIDE), BF16),
            pltpu.VMEM((40, C), F32),
            pltpu.VMEM((40, C // 2), F32),
            pltpu.VMEM((SEQ, 8, 128), F32),
            pltpu.VMEM((SEQ, 8, 128), F32),
            pltpu.VMEM((CHIPS, 8, 128), F32),
            pltpu.VMEM((2, SEQ, 8, 128), F32),
            dma((7,)), dma((2,)), dma((2,)),
            dma((DEPTH,)), dma((DEPTH,)), dma((RING,)), dma((RING,)), dma((DEPTH,)), dma((DEPTH,)),
            dma((RING,)), dma((RING,)), dma((DEPTH,)), dma((DEPTH,)),
            dma((2,)), dma((2,)), dma((3,)), dma((3,)),
        ],
        compiler_params=pltpu.CompilerParams(
            collective_id=0, has_side_effects=True, vmem_limit_bytes=60 * 2**20
        ),
        cost_estimate=pl.CostEstimate(
            flops=2_000_000_000, bytes_accessed=8_000_000, transcendentals=4_000_000
        ),
    )(
        dna_bases, conv_weight, conv_bias, w_query, w_key, w_value, out_grad,
    )


def solution(mesh):
    in_specs = (P("dp", "seq"), P(), P(), P(), P(), P(), P("dp", "seq", None))
    out_specs = (P("dp", "seq", None), P("dp", "seq", None), P(), P())
    return jax.shard_map(
        per_device, mesh=mesh, in_specs=in_specs, out_specs=out_specs, check_vma=False
    )
```

```python
import functools

import jax
import jax.numpy as jnp
from jax import lax
from jax.experimental import pallas as pl
from jax.experimental.pallas import tpu as pltpu
from jax.sharding import PartitionSpec as P

C = 1536
HEAD = 192
LETTERS = 5
POOL = 128
INNER = 768
ROWS = 8
SPAN = ROWS * POOL
CODES = 48
WIDE = 256
LANES = 512
DEPTH = 4
RING = 8
SEQ = DEPTH * RING
NEAR = 32
FAR = 32
GELU_A = 0.7978845608028654
GELU_B = 0.044715
NT = (((1,), (1,)), ((), ()))
MESH = pl.DeviceIdType.MESH
F32 = jnp.float32
BF16 = jnp.bfloat16


def bits(value, low, count):
    return lax.bitwise_and(lax.shift_right_logical(value, low), (1 << count) - 1)


def window_start(head):
    return 384 * (head // 2) + 128 * (head % 2)


def one_hot_rows(codes):
    width = codes.shape[1]
    wide = jnp.broadcast_to(codes, (8, width))
    letter = lax.broadcasted_iota(jnp.int32, (8, width - 256), 0)
    parts = []
    for tap in range(5):
        moved = wide if tap == 2 else pltpu.roll(wide, (2 - tap) % width, 1)
        hit = moved[:, 128 : width - 128] == letter
        if tap == 0:
            hit = jnp.logical_or(hit, letter >= LETTERS)
        parts.append(jnp.where(hit, 1.0, 0.0).astype(F32))
    parts.append(jnp.zeros_like(parts[0]))
    return jnp.concatenate(parts, axis=0)


def positions_first(rows):
    full = jnp.concatenate([rows, jnp.zeros((128 - CODES, rows.shape[1]), F32)], axis=0)
    blocks = [full[:, at : at + 128].T for at in range(0, rows.shape[1], 128)]
    return jnp.concatenate(blocks, axis=0)


def gelu_twice(x):
    square = x * x
    inner = x * (square * (GELU_A * GELU_B) + GELU_A)
    tanh = jnp.tanh(inner)
    return x + x * tanh, square, tanh


def gelu_slope_twice(x, square, tanh):
    return (1.0 + tanh) + (x - x * (tanh * tanh)) * (square * (3 * GELU_A * GELU_B) + GELU_A)


def stem_kernel(
    dna_hbm, taps_hbm, bias_hbm, wq_hbm, wk_hbm, wv_hbm, grad_hbm,
    attended_ref, pooled_ref, conv_ref, conv_bias_ref,
    dna_ref, taps_ref, bias_ref, grad_ref, weights, table, hot, hot_t, pooled_sum, slope_rows, slopes, halo,
    grad_send, grad_rows, grad_all, pool_rows, k_all, qv_all, back_send, back_rows,
    acc, chunks, near_rows, far_rows, full,
    load_sem, halo_ss, halo_rs, g1_ss, g1_rs, g2_ss, g2_rs, p_ss, p_rs, k_ss, k_rs, q_ss, q_rs, b_ss, b_rs,
    s_ss, s_rs,
):
    dp = lax.axis_index("dp")
    seq = lax.axis_index("seq")
    head, col = bits(seq, 3, 2), bits(seq, 0, 3)
    near = col * 4 + bits(dp, 0, 2)
    far = bits(dp, 2, 2) * 8 + bits(dp, 4, 1) * 4 + head

    def along_z(step):
        return (dp, lax.bitwise_and(seq + (step * RING + SEQ), SEQ - 1))

    def along_x(step):
        return (dp, head * RING + lax.bitwise_and(col + step, RING - 1))

    def along_seq(step):
        return (dp, lax.bitwise_and(seq + (step + SEQ), SEQ - 1))

    def device_at(near, far):
        return (
            bits(far, 2, 1) * 16 + bits(far, 3, 2) * 4 + bits(near, 0, 2),
            bits(far, 0, 2) * RING + bits(near, 2, 3),
        )

    def along_near(step):
        to = lax.bitwise_and(near + step, NEAR - 1)
        return to, device_at(to, far)

    def along_far(step):
        return device_at(near, lax.bitwise_and(far + step, FAR - 1))

    def remote(src, dst, ss, rs, device):
        return pltpu.make_async_remote_copy(
            src_ref=src, dst_ref=dst, send_sem=ss, recv_sem=rs, device_id=device, device_id_type=MESH
        )

    barrier = pltpu.get_barrier_semaphore()

    def greet(device):
        pl.semaphore_signal(barrier, inc=1, device_id=device, device_id_type=MESH)

    def greet_near(step, _):
        greet(along_near(step)[1])
        return 0

    def greet_far(step, _):
        greet(along_far(step))
        return 0

    greet(along_seq(1))
    greet(along_seq(-1))
    for step in (2, 1, 3):
        greet(along_z(step))
    for step in range(1, RING):
        greet(along_x(step))
    lax.fori_loop(1, NEAR, greet_near, 0)
    lax.fori_loop(1, FAR, greet_far, 0)


    small = ((dna_hbm, dna_ref), (taps_hbm, taps_ref), (bias_hbm, bias_ref), (grad_hbm, grad_ref))
    reads = [pltpu.make_async_copy(hbm, ref, load_sem.at[3 + i]) for i, (hbm, ref) in enumerate(small)]
    loads = [
        pltpu.make_async_copy(hbm, weights.at[i], load_sem.at[i])
        for i, hbm in enumerate((wq_hbm, wk_hbm, wv_hbm))
    ]
    for copy in (*reads, *loads):
        copy.start()

    for copy in reads:
        copy.wait()

    bias = bias_ref[...].reshape(1, C)
    bias_high = bias.astype(BF16).astype(F32)
    bias_mid = (bias - bias_high).astype(BF16).astype(F32)
    bias_low = bias - bias_high - bias_mid
    for tap in range(5):
        letters = taps_ref[tap].astype(F32)
        spare = [bias_high, bias_mid, bias_low] if tap == 0 else [jnp.zeros((3, C), F32)]
        pair = jnp.concatenate([letters, *spare], axis=0)
        acc[8 * tap : 8 * tap + 8, :] = pair
    table[0:48, :] = jnp.concatenate([acc[...], jnp.zeros((8, C), F32)], axis=0).astype(BF16)
    table[48:128, :] = jnp.zeros((80, C), BF16)

    codes = dna_ref[...]
    outside = jnp.full((1, 128), -1, jnp.int32)
    rows = one_hot_rows(jnp.concatenate([outside, codes, outside], axis=1))
    hot_t[...] = rows.astype(BF16)
    hot[...] = positions_first(rows).astype(BF16)

    def pre_act(block, lanes):
        return jnp.dot(
            hot[block * POOL : (block + 1) * POOL, :], table[:, lanes], preferred_element_type=F32
        )

    def lanes_of(part):
        return pl.ds(pl.multiple_of(part * LANES, LANES), LANES)

    def pools(blocks):
        def body(part, _):
            lanes = lanes_of(part)
            for block in blocks:
                twice, _, _ = gelu_twice(pre_act(block, lanes))
                pooled_sum[block : block + 1, lanes] = jnp.sum(twice, axis=0, keepdims=True)
            return 0

        return body

    inner, ends = pools(range(1, ROWS - 1)), pools((0, ROWS - 1))

    def slope_part(part, _):
        lanes = lanes_of(part)
        for block in range(ROWS):
            x = pre_act(block, lanes)
            _, square, tanh = gelu_twice(x)
            slope = gelu_slope_twice(x, square, tanh)
            slope_rows[block * POOL : (block + 1) * POOL, lanes] = slope.astype(BF16)
        return 0

    lane = lax.broadcasted_iota(jnp.int32, (ROWS, WIDE), 1)
    grad = grad_ref[0].astype(F32)
    for h in range(DEPTH):
        low = 64 * (h % 2)
        start = window_start(h)
        keep = jnp.logical_and(lane >= low, lane < low + HEAD)
        window = jnp.where(keep, grad[:, start : start + WIDE], 0.0)
        if h % 2 == 0:
            window = pltpu.roll(window, 64, 1)
        grad_send[h] = jnp.concatenate([window[:, :128], window[:, 128:]], axis=0).astype(BF16)

    lax.fori_loop(0, 1, inner, 0)
    pl.semaphore_wait(barrier, 2 + (DEPTH - 1) + (RING - 1) + (NEAR - 1) + (FAR - 1))

    halo_sends = [
        remote(dna_ref.at[:, SPAN - 128 : SPAN], halo.at[0], halo_ss.at[0], halo_rs.at[0], along_seq(1)),
        remote(dna_ref.at[:, 0:128], halo.at[1], halo_ss.at[1], halo_rs.at[1], along_seq(-1)),
    ]
    for copy in halo_sends:
        copy.start()
    g1 = [
        remote(
            grad_send.at[lax.bitwise_and(head + step, DEPTH - 1)], grad_rows.at[step],
            g1_ss.at[step], g1_rs.at[step], along_z(step),
        )
        for step in range(1, DEPTH)
    ]
    for copy in g1:
        copy.start()
    grad_rows[0] = grad_send[head]

    lax.fori_loop(1, C // LANES, inner, 0)

    for copy in halo_sends:
        copy.wait()
    before = jnp.where(seq == 0, -1, halo[0])
    after = jnp.where(seq == SEQ - 1, -1, halo[1])
    first = one_hot_rows(jnp.concatenate([before, codes[:, :256]], axis=1))
    last = one_hot_rows(jnp.concatenate([codes[:, SPAN - 256 :], after], axis=1))
    hot_t[:, :POOL] = first.astype(BF16)
    hot_t[:, SPAN - POOL :] = last.astype(BF16)
    hot[:POOL, :] = positions_first(first).astype(BF16)
    hot[SPAN - POOL :, :] = positions_first(last).astype(BF16)
    lax.fori_loop(0, C // LANES, ends, 0)

    pooled = pooled_sum[...] * (0.5 / POOL)
    pooled_ref[0] = pooled.astype(BF16)
    pool_rows[0] = jnp.concatenate([pooled[:, :INNER], pooled[:, INNER:]], axis=0).astype(BF16)
    p1 = [
        remote(pool_rows.at[0], pool_rows.at[step], p_ss.at[step], p_rs.at[step], along_z(step))
        for step in range(1, DEPTH)
    ]
    for copy in p1:
        copy.start()

    for copy in g1:
        copy.wait()
    blocks = grad_rows[...].astype(F32)
    grad_all[0] = jnp.concatenate(
        [jnp.concatenate([blocks[i, :8], blocks[i, 8:]], axis=1) for i in range(DEPTH)], axis=0
    ).astype(BF16)
    g2 = [
        remote(grad_all.at[0], grad_all.at[step], g2_ss.at[step], g2_rs.at[step], along_x(step))
        for step in range(1, RING)
    ]
    for copy in g2:
        copy.start()

    lax.fori_loop(0, C // LANES - 1, slope_part, 0)

    for load in loads:
        load.wait()
    for copy in p1:
        copy.wait()
    odd = bits(head, 0, 1)
    start = pl.multiple_of(384 * bits(head, 1, 1) + 128 * odd, 128)
    low = 64 * odd
    lane = lax.broadcasted_iota(jnp.int32, (4 * ROWS, WIDE), 1)
    keep = jnp.logical_and(lane >= low, lane < low + HEAD)
    halves = pool_rows[...].reshape(DEPTH * 16, INNER)

    def projected(i):
        left = jnp.dot(halves, weights[i, :INNER, pl.ds(start, WIDE)], preferred_element_type=F32)
        right = jnp.dot(halves, weights[i, INNER:, pl.ds(start, WIDE)], preferred_element_type=F32)
        rows = jnp.concatenate(
            [left[16 * j : 16 * j + 8] + right[16 * j + 8 : 16 * j + 16] for j in range(DEPTH)], axis=0
        )
        return pltpu.roll(jnp.where(keep, rows, 0.0), 192 * odd, 1)

    def round_x(ref, ss, rs):
        copies = [
            remote(ref.at[0], ref.at[step], ss.at[step], rs.at[step], along_x(step))
            for step in (4, 3, 5, 2, 6, 1, 7)
        ]
        for copy in copies:
            copy.start()
        return copies

    k_all[0] = projected(1).astype(BF16)
    k1 = round_x(k_all, k_ss, k_rs)
    query, value = projected(0), pltpu.roll(projected(2), 64, 1)
    qv_all[0] = jnp.concatenate(
        [query[:, :128], query[:, 128:] + value[:, :128], value[:, 128:]], axis=1
    ).astype(BF16)
    q1 = round_x(qv_all, q_ss, q_rs) + k1
    lax.fori_loop(C // LANES - 1, C // LANES, slope_part, 0)
    for block in range(ROWS):
        rows = slice(block * POOL, (block + 1) * POOL)
        slopes[block] = jnp.dot(hot_t[:, rows], slope_rows[rows, :], preferred_element_type=F32)
    for copy in g2:
        copy.wait()
    for copy in q1:
        copy.wait()

    everyone = RING * 32
    q = qv_all[:, :, :WIDE].reshape(everyone, WIDE)
    v = qv_all[:, :, 128:].reshape(everyone, WIDE)
    k = k_all[...].reshape(everyone, WIDE)
    g = grad_all[...].reshape(everyone, WIDE)
    scale = HEAD ** (-0.5)

    def soft_parts(scores, d_soft, axis):
        scores = scores * scale
        shifted = jnp.exp(scores - jnp.max(scores, axis=axis, keepdims=True))
        soft = shifted / jnp.sum(shifted, axis=axis, keepdims=True)
        delta = jnp.sum(soft * d_soft, axis=axis, keepdims=True)
        return soft, delta

    def finish(soft, d_soft, delta):
        return soft.astype(BF16), (soft * (d_soft - delta) * scale).astype(BF16)

    scores_t = lax.dot_general(k, q, NT, preferred_element_type=F32)
    d_soft_t = lax.dot_general(v, g, NT, preferred_element_type=F32)
    scores_own = lax.dot_general(q[:32], k, NT, preferred_element_type=F32)
    d_soft_own = lax.dot_general(g[:32], v, NT, preferred_element_type=F32)
    soft_t, delta_t = soft_parts(scores_t, d_soft_t, 0)
    half_t, d_half_t = finish(soft_t[:32], d_soft_t[:32], delta_t)
    soft_own, delta_own = soft_parts(scores_own, d_soft_own, 1)
    half_own, d_half_own = finish(soft_own, d_soft_own, delta_own)
    results = (
        jnp.dot(half_own, v, preferred_element_type=F32),
        jnp.dot(d_half_own, k, preferred_element_type=F32),
        jnp.dot(d_half_t, q, preferred_element_type=F32),
        jnp.dot(half_t, g, preferred_element_type=F32),
    )
    low_side, high_side = 64 * odd, 192 * (1 - odd)
    results = (
        pltpu.roll(jnp.where(lane >= 64, results[0], 0.0), high_side, 1),
        pltpu.roll(results[1], low_side, 1),
        pltpu.roll(jnp.where(lane < HEAD, results[2], 0.0), low_side, 1),
        pltpu.roll(results[3], high_side, 1),
    )
    for i in range(DEPTH):
        mine = jnp.concatenate([result[8 * i : 8 * i + 8] for result in results], axis=0).astype(BF16)
        if i == 0:
            back_rows[0] = mine
        else:
            back_send[i] = mine
    b1 = [
        remote(back_send.at[i], back_rows.at[i], b_ss.at[i], b_rs.at[i], along_z(-i))
        for i in range(1, DEPTH)
    ]
    for copy in b1:
        copy.start()
    for copy in b1:
        copy.wait()

    by_head = [back_rows[lax.bitwise_and(h - head + DEPTH, DEPTH - 1)].astype(F32) for h in range(DEPTH)]

    def joined(i):
        a, b, c, d = (rows[8 * i : 8 * i + 8] for rows in by_head)
        return jnp.concatenate(
            [a[:, :128], a[:, 128:] + b[:, :128], b[:, 128:], c[:, :128], c[:, 128:] + d[:, :128], d[:, 128:]],
            axis=1,
        ).astype(BF16)

    attended_ref[0] = joined(0)
    d_pooled = lax.dot_general(joined(1), weights[0], NT, preferred_element_type=F32)
    d_pooled += lax.dot_general(joined(2), weights[1], NT, preferred_element_type=F32)
    d_pooled += lax.dot_general(joined(3), weights[2], NT, preferred_element_type=F32)
    d_pooled *= 0.5 / POOL
    total = slopes[0, 0:40, :] * d_pooled[0:1]
    for block in range(1, ROWS):
        total += slopes[block, 0:40, :] * d_pooled[block : block + 1]
    for tap in range(5):
        for part in range(6):
            rows, at = slice(8 * tap, 8 * tap + 8), 256 * part
            chunk = [total[rows, at : at + 128], total[rows, at + 128 : at + 256]]
            chunks[6 * tap + part] = jnp.concatenate(chunk, axis=0).astype(BF16)
    chunks[30:32] = jnp.zeros((2, 16, 128), BF16)

    def scatter(step, _):
        to, device = along_near(step)
        remote(chunks.at[to], near_rows.at[step], s_ss.at[0], s_rs.at[0], device).start()
        return 0

    def spread(step, _):
        remote(far_rows.at[0], far_rows.at[step], s_ss.at[1], s_rs.at[1], along_far(step)).start()
        return 0

    def gather(step, _):
        mine = full.at[near]
        remote(mine, mine, s_ss.at[2], s_rs.at[2], along_near(step)[1]).start()
        return 0

    def wait_all(ref, at):
        remote(ref, ref, s_ss.at[at], s_rs.at[at], along_z(1)).wait()

    lax.fori_loop(1, NEAR, scatter, 0)
    wait_all(near_rows.at[1:NEAR], 0)
    near_sum = chunks[near].astype(F32) + jnp.sum(near_rows[1:NEAR].astype(F32), axis=0)
    far_rows[0] = near_sum.astype(BF16)
    lax.fori_loop(1, FAR, spread, 0)
    wait_all(far_rows.at[1:FAR], 1)
    far_sum = far_rows[far].astype(F32)
    for i in range(1, FAR):
        far_sum += far_rows[lax.bitwise_and(far + (FAR - i), FAR - 1)].astype(F32)
    full[near] = far_sum.astype(BF16)
    lax.fori_loop(1, NEAR, gather, 0)
    wait_all(full.at[0 : NEAR - 1], 2)
    for tap in range(5):
        for part in range(6):
            chunk = full[6 * tap + part].astype(F32)
            for side in range(2):
                lanes = slice(256 * part + 128 * side, 256 * part + 128 * side + 128)
                conv_ref[tap, :, lanes] = chunk[8 * side : 8 * side + LETTERS]
                if tap == 0:
                    conv_bias_ref[lanes] = chunk[8 * side + LETTERS]


def write_kernel(*refs):
    count = len(refs) // 2
    sems = refs[-1]
    copies = [pltpu.make_async_copy(refs[i], refs[count + i], sems.at[i]) for i in range(count)]
    for copy in copies:
        copy.start()
    for copy in copies:
        copy.wait()


def per_device(dna_bases, conv_weight, conv_bias, w_query, w_key, w_value, out_grad):
    vmem = pl.BlockSpec(memory_space=pltpu.VMEM)
    hbm = pl.BlockSpec(memory_space=pltpu.HBM)
    dma = pltpu.SemaphoreType.DMA
    results = pl.pallas_call(
        stem_kernel,
        name="genomic_stem",
        out_shape=(
            jax.ShapeDtypeStruct((1, ROWS, INNER), BF16),
            jax.ShapeDtypeStruct((1, ROWS, C), BF16),
            jax.ShapeDtypeStruct((5, LETTERS, C), F32),
            jax.ShapeDtypeStruct((C,), F32),
        ),
        in_specs=[hbm] * 7,
        out_specs=(vmem, vmem, vmem, vmem),
        scratch_shapes=[
            pltpu.VMEM((1, SPAN), jnp.int32),
            pltpu.VMEM((5, LETTERS, C), BF16),
            pltpu.VMEM((C,), F32),
            pltpu.VMEM((1, ROWS, INNER), BF16),
            pltpu.VMEM((3, C, INNER), BF16),
            pltpu.VMEM((128, C), BF16),
            pltpu.VMEM((SPAN, 128), BF16),
            pltpu.VMEM((CODES, SPAN), BF16),
            pltpu.VMEM((ROWS, C), F32),
            pltpu.VMEM((SPAN, C), BF16),
            pltpu.VMEM((ROWS, CODES, C), F32),
            pltpu.VMEM((2, 1, 128), jnp.int32),
            pltpu.VMEM((DEPTH, 16, 128), BF16),
            pltpu.VMEM((DEPTH, 16, 128), BF16),
            pltpu.VMEM((RING, 32, WIDE), BF16),
            pltpu.VMEM((DEPTH, 16, INNER), BF16),
            pltpu.VMEM((RING, 32, WIDE), BF16),
            pltpu.VMEM((RING, 32, 384), BF16),
            pltpu.VMEM((DEPTH, 32, WIDE), BF16),
            pltpu.VMEM((DEPTH, 32, WIDE), BF16),
            pltpu.VMEM((40, C), F32),
            pltpu.VMEM((NEAR, 16, 128), BF16),
            pltpu.VMEM((NEAR, 16, 128), BF16),
            pltpu.VMEM((FAR, 16, 128), BF16),
            pltpu.VMEM((NEAR, 16, 128), BF16),
            dma((7,)), dma((2,)), dma((2,)),
            dma((DEPTH,)), dma((DEPTH,)), dma((RING,)), dma((RING,)), dma((DEPTH,)), dma((DEPTH,)),
            dma((RING,)), dma((RING,)), dma((RING,)), dma((RING,)), dma((DEPTH,)), dma((DEPTH,)),
            dma((3,)), dma((3,)),
        ],
        compiler_params=pltpu.CompilerParams(
            collective_id=0, has_side_effects=True, vmem_limit_bytes=48 * 2**20
        ),
        cost_estimate=pl.CostEstimate(
            flops=2_000_000_000, bytes_accessed=8_000_000, transcendentals=4_000_000
        ),
    )(
        *(pltpu.with_memory_space_constraint(a, pltpu.HBM) for a in (
        dna_bases, conv_weight, conv_bias, w_query, w_key, w_value, out_grad))
    )
    return pl.pallas_call(
        write_kernel,
        name="write_results",
        out_shape=tuple(jax.ShapeDtypeStruct(a.shape, a.dtype) for a in results),
        in_specs=[vmem] * 4,
        out_specs=(hbm,) * 4,
        scratch_shapes=[dma((4,))],
        compiler_params=pltpu.CompilerParams(vmem_limit_bytes=2**20),
    )(*results)


def solution(mesh):
    in_specs = (P("dp", "seq"), P(), P(), P(), P(), P(), P("dp", "seq", None))
    out_specs = (P("dp", "seq", None), P("dp", "seq", None), P(), P())
    return jax.shard_map(
        per_device, mesh=mesh, in_specs=in_specs, out_specs=out_specs, check_vma=False
    )
```

```python
import functools

import jax
import jax.numpy as jnp
from jax import lax
from jax.experimental import pallas as pl
from jax.experimental.pallas import tpu as pltpu
from jax.sharding import PartitionSpec as P

C = 1536
HEAD = 192
LETTERS = 5
POOL = 128
INNER = 768
ROWS = 8
SPAN = ROWS * POOL
CODES = 48
WIDE = 256
LANES = 512
DEPTH = 4
RING = 8
SEQ = DEPTH * RING
NEAR = 32
FAR = 32
GELU_A = 0.7978845608028654
GELU_B = 0.044715
NT = (((1,), (1,)), ((), ()))
MESH = pl.DeviceIdType.MESH
F32 = jnp.float32
BF16 = jnp.bfloat16


def bits(value, low, count):
    return lax.bitwise_and(lax.shift_right_logical(value, low), (1 << count) - 1)


def window_start(head):
    return 384 * (head // 2) + 128 * (head % 2)


def one_hot_rows(codes):
    width = codes.shape[1]
    wide = jnp.broadcast_to(codes, (8, width))
    letter = lax.broadcasted_iota(jnp.int32, (8, width - 256), 0)
    parts = []
    for tap in range(5):
        moved = wide if tap == 2 else pltpu.roll(wide, (2 - tap) % width, 1)
        hit = moved[:, 128 : width - 128] == letter
        if tap == 0:
            hit = jnp.logical_or(hit, letter >= LETTERS)
        parts.append(jnp.where(hit, 1.0, 0.0).astype(F32))
    parts.append(jnp.zeros_like(parts[0]))
    return jnp.concatenate(parts, axis=0)


def positions_first(rows):
    full = jnp.concatenate([rows, jnp.zeros((128 - CODES, rows.shape[1]), F32)], axis=0)
    blocks = [full[:, at : at + 128].T for at in range(0, rows.shape[1], 128)]
    return jnp.concatenate(blocks, axis=0)


def gelu_twice(x):
    square = x * x
    inner = x * (square * (GELU_A * GELU_B) + GELU_A)
    tanh = jnp.tanh(inner)
    return x + x * tanh, square, tanh


def gelu_slope_twice(x, square, tanh):
    return (1.0 + tanh) + (x - x * (tanh * tanh)) * (square * (3 * GELU_A * GELU_B) + GELU_A)


def stem_kernel(
    dna_hbm, taps_hbm, bias_hbm, wq_hbm, wk_hbm, wv_hbm, grad_hbm,
    attended_ref, pooled_ref, conv_ref, conv_bias_ref,
    dna_ref, taps_ref, bias_ref, grad_ref, weights, table, hot, hot_t, pooled_sum, slope_rows, slopes, halo,
    grad_send, grad_rows, grad_all, pool_rows, k_all, qv_all, back_send, back_rows,
    acc, chunks, near_rows, far_rows, full,
    met_sem, load_sem, halo_ss, halo_rs, g1_ss, g1_rs, g2_ss, g2_rs, p_ss, p_rs, k_ss, k_rs, q_ss, q_rs, b_ss, b_rs,
    s_ss, s_rs,
):
    dp = lax.axis_index("dp")
    seq = lax.axis_index("seq")
    head, col = bits(seq, 3, 2), bits(seq, 0, 3)
    near = col * 4 + bits(dp, 0, 2)
    far = bits(dp, 2, 2) * 8 + bits(dp, 4, 1) * 4 + head

    def along_z(step):
        return (dp, lax.bitwise_and(seq + (step * RING + SEQ), SEQ - 1))

    def along_x(step):
        return (dp, head * RING + lax.bitwise_and(col + step, RING - 1))

    def along_seq(step):
        return (dp, lax.bitwise_and(seq + (step + SEQ), SEQ - 1))

    def device_at(near, far):
        return (
            bits(far, 2, 1) * 16 + bits(far, 3, 2) * 4 + bits(near, 0, 2),
            bits(far, 0, 2) * RING + bits(near, 2, 3),
        )

    def along_near(step):
        to = lax.bitwise_and(near + step, NEAR - 1)
        return to, device_at(to, far)

    def along_far(step):
        return device_at(near, lax.bitwise_and(far + step, FAR - 1))

    def remote(src, dst, ss, rs, device):
        return pltpu.make_async_remote_copy(
            src_ref=src, dst_ref=dst, send_sem=ss, recv_sem=rs, device_id=device, device_id_type=MESH
        )

    other_core = (dp + 1 - 2 * bits(dp, 0, 1), seq)
    other_y = (dp + 2 - 4 * bits(dp, 1, 1), seq)
    other_half = (dp + 16 - 32 * bits(dp, 4, 1), seq)
    quad = bits(dp, 2, 2)
    pairs_y = [(dp + 4 * (lax.bitwise_and(quad + step, 3) - quad), seq) for step in (1, 2, 3)]
    column = [along_z(step) for step in range(1, DEPTH)]
    first_met = [
        along_seq(1), along_seq(-1), *column, *(along_x(step) for step in (4, 3, 5, 2, 6, 1, 7)),
        other_half, *pairs_y, other_y, other_core,
    ]
    barrier = pltpu.get_barrier_semaphore()
    for device in first_met:
        pl.semaphore_signal(barrier, inc=1, device_id=device, device_id_type=MESH)

    def tell(at, devices):
        for device in devices:
            pl.semaphore_signal(met_sem.at[at], inc=1, device_id=device, device_id_type=MESH)

    small = ((dna_hbm, dna_ref), (taps_hbm, taps_ref), (bias_hbm, bias_ref), (grad_hbm, grad_ref))
    reads = [pltpu.make_async_copy(hbm, ref, load_sem.at[3 + i]) for i, (hbm, ref) in enumerate(small)]
    loads = [
        pltpu.make_async_copy(hbm, weights.at[i], load_sem.at[i])
        for i, hbm in enumerate((wq_hbm, wk_hbm, wv_hbm))
    ]
    for copy in (*reads, *loads):
        copy.start()

    for copy in reads:
        copy.wait()

    bias = bias_ref[...].reshape(1, C)
    bias_high = bias.astype(BF16).astype(F32)
    bias_mid = (bias - bias_high).astype(BF16).astype(F32)
    bias_low = bias - bias_high - bias_mid
    for tap in range(5):
        letters = taps_ref[tap].astype(F32)
        spare = [bias_high, bias_mid, bias_low] if tap == 0 else [jnp.zeros((3, C), F32)]
        pair = jnp.concatenate([letters, *spare], axis=0)
        acc[8 * tap : 8 * tap + 8, :] = pair
    table[0:48, :] = jnp.concatenate([acc[...], jnp.zeros((8, C), F32)], axis=0).astype(BF16)
    table[48:128, :] = jnp.zeros((80, C), BF16)

    codes = dna_ref[...]
    outside = jnp.full((1, 128), -1, jnp.int32)
    rows = one_hot_rows(jnp.concatenate([outside, codes, outside], axis=1))
    hot_t[...] = rows.astype(BF16)
    hot[...] = positions_first(rows).astype(BF16)

    def pre_act(block, lanes):
        return jnp.dot(
            hot[block * POOL : (block + 1) * POOL, :], table[:, lanes], preferred_element_type=F32
        )

    def lanes_of(part):
        return pl.ds(pl.multiple_of(part * LANES, LANES), LANES)

    def pools(blocks):
        def body(part, _):
            lanes = lanes_of(part)
            for block in blocks:
                twice, _, _ = gelu_twice(pre_act(block, lanes))
                pooled_sum[block : block + 1, lanes] = jnp.sum(twice, axis=0, keepdims=True)
            return 0

        return body

    inner, ends = pools(range(1, ROWS - 1)), pools((0, ROWS - 1))

    def slope_part(part, _):
        lanes = lanes_of(part)
        for block in range(ROWS):
            x = pre_act(block, lanes)
            _, square, tanh = gelu_twice(x)
            slope = gelu_slope_twice(x, square, tanh)
            slope_rows[block * POOL : (block + 1) * POOL, lanes] = slope.astype(BF16)
        return 0

    lane = lax.broadcasted_iota(jnp.int32, (ROWS, WIDE), 1)
    grad = grad_ref[0].astype(F32)
    for h in range(DEPTH):
        low = 64 * (h % 2)
        start = window_start(h)
        keep = jnp.logical_and(lane >= low, lane < low + HEAD)
        window = jnp.where(keep, grad[:, start : start + WIDE], 0.0)
        if h % 2 == 0:
            window = pltpu.roll(window, 64, 1)
        grad_send[h] = jnp.concatenate([window[:, :128], window[:, 128:]], axis=0).astype(BF16)

    lax.fori_loop(0, 1, inner, 0)
    pl.semaphore_wait(barrier, len(first_met))

    halo_sends = [
        remote(dna_ref.at[:, SPAN - 128 : SPAN], halo.at[0], halo_ss.at[0], halo_rs.at[0], along_seq(1)),
        remote(dna_ref.at[:, 0:128], halo.at[1], halo_ss.at[1], halo_rs.at[1], along_seq(-1)),
    ]
    for copy in halo_sends:
        copy.start()
    g1 = [
        remote(
            grad_send.at[lax.bitwise_and(head + step, DEPTH - 1)], grad_rows.at[step],
            g1_ss.at[step], g1_rs.at[step], along_z(step),
        )
        for step in range(1, DEPTH)
    ]
    for copy in g1:
        copy.start()
    grad_rows[0] = grad_send[head]
    tell(0, (other_core, other_y, other_half, *column))

    lax.fori_loop(1, C // LANES, inner, 0)

    for copy in halo_sends:
        copy.wait()
    before = jnp.where(seq == 0, -1, halo[0])
    after = jnp.where(seq == SEQ - 1, -1, halo[1])
    first = one_hot_rows(jnp.concatenate([before, codes[:, :256]], axis=1))
    last = one_hot_rows(jnp.concatenate([codes[:, SPAN - 256 :], after], axis=1))
    hot_t[:, :POOL] = first.astype(BF16)
    hot_t[:, SPAN - POOL :] = last.astype(BF16)
    hot[:POOL, :] = positions_first(first).astype(BF16)
    hot[SPAN - POOL :, :] = positions_first(last).astype(BF16)
    lax.fori_loop(0, C // LANES, ends, 0)

    pooled = pooled_sum[...] * (0.5 / POOL)
    pooled_ref[0] = pooled.astype(BF16)
    pool_rows[0] = jnp.concatenate([pooled[:, :INNER], pooled[:, INNER:]], axis=0).astype(BF16)
    p1 = [
        remote(pool_rows.at[0], pool_rows.at[step], p_ss.at[step], p_rs.at[step], along_z(step))
        for step in range(1, DEPTH)
    ]
    for copy in p1:
        copy.start()

    for copy in g1:
        copy.wait()
    blocks = grad_rows[...].astype(F32)
    grad_all[0] = jnp.concatenate(
        [jnp.concatenate([blocks[i, :8], blocks[i, 8:]], axis=1) for i in range(DEPTH)], axis=0
    ).astype(BF16)
    g2 = [
        remote(grad_all.at[0], grad_all.at[step], g2_ss.at[step], g2_rs.at[step], along_x(step))
        for step in range(1, RING)
    ]
    for copy in g2:
        copy.start()

    lax.fori_loop(0, C // LANES - 1, slope_part, 0)

    for load in loads:
        load.wait()
    for copy in p1:
        copy.wait()
    pl.semaphore_wait(met_sem.at[0], 6)
    tell(1, (other_core, other_half))
    odd = bits(head, 0, 1)
    start = pl.multiple_of(384 * bits(head, 1, 1) + 128 * odd, 128)
    low = 64 * odd
    lane = lax.broadcasted_iota(jnp.int32, (4 * ROWS, WIDE), 1)
    keep = jnp.logical_and(lane >= low, lane < low + HEAD)
    halves = pool_rows[...].reshape(DEPTH * 16, INNER)

    def projected(i):
        left = jnp.dot(halves, weights[i, :INNER, pl.ds(start, WIDE)], preferred_element_type=F32)
        right = jnp.dot(halves, weights[i, INNER:, pl.ds(start, WIDE)], preferred_element_type=F32)
        rows = jnp.concatenate(
            [left[16 * j : 16 * j + 8] + right[16 * j + 8 : 16 * j + 16] for j in range(DEPTH)], axis=0
        )
        return pltpu.roll(jnp.where(keep, rows, 0.0), 192 * odd, 1)

    def round_x(ref, ss, rs):
        copies = [
            remote(ref.at[0], ref.at[step], ss.at[step], rs.at[step], along_x(step))
            for step in (4, 3, 5, 2, 6, 1, 7)
        ]
        for copy in copies:
            copy.start()
        return copies

    k_all[0] = projected(1).astype(BF16)
    k1 = round_x(k_all, k_ss, k_rs)
    query, value = projected(0), pltpu.roll(projected(2), 64, 1)
    qv_all[0] = jnp.concatenate(
        [query[:, :128], query[:, 128:] + value[:, :128], value[:, 128:]], axis=1
    ).astype(BF16)
    q1 = round_x(qv_all, q_ss, q_rs) + k1
    lax.fori_loop(C // LANES - 1, C // LANES, slope_part, 0)
    for block in range(ROWS):
        rows = slice(block * POOL, (block + 1) * POOL)
        slopes[block] = jnp.dot(hot_t[:, rows], slope_rows[rows, :], preferred_element_type=F32)
    for copy in g2:
        copy.wait()
    for copy in q1:
        copy.wait()

    everyone = RING * 32
    q = qv_all[:, :, :WIDE].reshape(everyone, WIDE)
    v = qv_all[:, :, 128:].reshape(everyone, WIDE)
    k = k_all[...].reshape(everyone, WIDE)
    g = grad_all[...].reshape(everyone, WIDE)
    scale = HEAD ** (-0.5)

    def soft_parts(scores, d_soft, axis):
        scores = scores * scale
        shifted = jnp.exp(scores - jnp.max(scores, axis=axis, keepdims=True))
        soft = shifted / jnp.sum(shifted, axis=axis, keepdims=True)
        delta = jnp.sum(soft * d_soft, axis=axis, keepdims=True)
        return soft, delta

    def finish(soft, d_soft, delta):
        return soft.astype(BF16), (soft * (d_soft - delta) * scale).astype(BF16)

    scores_t = lax.dot_general(k, q, NT, preferred_element_type=F32)
    d_soft_t = lax.dot_general(v, g, NT, preferred_element_type=F32)
    scores_own = lax.dot_general(q[:32], k, NT, preferred_element_type=F32)
    d_soft_own = lax.dot_general(g[:32], v, NT, preferred_element_type=F32)
    soft_t, delta_t = soft_parts(scores_t, d_soft_t, 0)
    half_t, d_half_t = finish(soft_t[:32], d_soft_t[:32], delta_t)
    soft_own, delta_own = soft_parts(scores_own, d_soft_own, 1)
    half_own, d_half_own = finish(soft_own, d_soft_own, delta_own)
    results = (
        jnp.dot(half_own, v, preferred_element_type=F32),
        jnp.dot(d_half_own, k, preferred_element_type=F32),
        jnp.dot(d_half_t, q, preferred_element_type=F32),
        jnp.dot(half_t, g, preferred_element_type=F32),
    )
    low_side, high_side = 64 * odd, 192 * (1 - odd)
    results = (
        pltpu.roll(jnp.where(lane >= 64, results[0], 0.0), high_side, 1),
        pltpu.roll(results[1], low_side, 1),
        pltpu.roll(jnp.where(lane < HEAD, results[2], 0.0), low_side, 1),
        pltpu.roll(results[3], high_side, 1),
    )
    for i in range(DEPTH):
        mine = jnp.concatenate([result[8 * i : 8 * i + 8] for result in results], axis=0).astype(BF16)
        if i == 0:
            back_rows[0] = mine
        else:
            back_send[i] = mine
    b1 = [
        remote(back_send.at[i], back_rows.at[i], b_ss.at[i], b_rs.at[i], along_z(-i))
        for i in range(1, DEPTH)
    ]
    for copy in b1:
        copy.start()
    for copy in b1:
        copy.wait()

    by_head = [back_rows[lax.bitwise_and(h - head + DEPTH, DEPTH - 1)].astype(F32) for h in range(DEPTH)]

    def joined(i):
        a, b, c, d = (rows[8 * i : 8 * i + 8] for rows in by_head)
        return jnp.concatenate(
            [a[:, :128], a[:, 128:] + b[:, :128], b[:, 128:], c[:, :128], c[:, 128:] + d[:, :128], d[:, 128:]],
            axis=1,
        ).astype(BF16)

    attended_ref[0] = joined(0)
    d_pooled = lax.dot_general(joined(1), weights[0], NT, preferred_element_type=F32)
    d_pooled += lax.dot_general(joined(2), weights[1], NT, preferred_element_type=F32)
    d_pooled += lax.dot_general(joined(3), weights[2], NT, preferred_element_type=F32)
    d_pooled *= 0.5 / POOL
    total = slopes[0, 0:40, :] * d_pooled[0:1]
    for block in range(1, ROWS):
        total += slopes[block, 0:40, :] * d_pooled[block : block + 1]
    for tap in range(5):
        for part in range(6):
            rows, at = slice(8 * tap, 8 * tap + 8), 256 * part
            chunk = [total[rows, at : at + 128], total[rows, at + 128 : at + 256]]
            chunks[6 * tap + part] = jnp.concatenate(chunk, axis=0).astype(BF16)
    chunks[30:32] = jnp.zeros((2, 16, 128), BF16)

    def scatter(step, _):
        to, device = along_near(step)
        remote(chunks.at[to], near_rows.at[step], s_ss.at[0], s_rs.at[0], device).start()
        return 0

    def spread(step, _):
        remote(far_rows.at[0], far_rows.at[step], s_ss.at[1], s_rs.at[1], along_far(step)).start()
        return 0

    def gather(step, _):
        mine = full.at[near]
        remote(mine, mine, s_ss.at[2], s_rs.at[2], along_near(step)[1]).start()
        return 0

    def wait_all(ref, at):
        remote(ref, ref, s_ss.at[at], s_rs.at[at], along_z(1)).wait()

    pl.semaphore_wait(met_sem.at[1], 2)
    lax.fori_loop(1, NEAR, scatter, 0)
    wait_all(near_rows.at[1:NEAR], 0)
    near_sum = chunks[near].astype(F32) + jnp.sum(near_rows[1:NEAR].astype(F32), axis=0)
    far_rows[0] = near_sum.astype(BF16)
    lax.fori_loop(1, FAR, spread, 0)
    wait_all(far_rows.at[1:FAR], 1)
    far_sum = far_rows[far].astype(F32)
    for i in range(1, FAR):
        far_sum += far_rows[lax.bitwise_and(far + (FAR - i), FAR - 1)].astype(F32)
    full[near] = far_sum.astype(BF16)
    lax.fori_loop(1, NEAR, gather, 0)
    wait_all(full.at[0 : NEAR - 1], 2)
    for tap in range(5):
        for part in range(6):
            chunk = full[6 * tap + part].astype(F32)
            for side in range(2):
                lanes = slice(256 * part + 128 * side, 256 * part + 128 * side + 128)
                conv_ref[tap, :, lanes] = chunk[8 * side : 8 * side + LETTERS]
                if tap == 0:
                    conv_bias_ref[lanes] = chunk[8 * side + LETTERS]


def write_kernel(*refs):
    count = len(refs) // 2
    sems = refs[-1]
    copies = [pltpu.make_async_copy(refs[i], refs[count + i], sems.at[i]) for i in range(count)]
    for copy in copies:
        copy.start()
    for copy in copies:
        copy.wait()


def per_device(dna_bases, conv_weight, conv_bias, w_query, w_key, w_value, out_grad):
    vmem = pl.BlockSpec(memory_space=pltpu.VMEM)
    hbm = pl.BlockSpec(memory_space=pltpu.HBM)
    dma = pltpu.SemaphoreType.DMA
    results = pl.pallas_call(
        stem_kernel,
        name="genomic_stem",
        out_shape=(
            jax.ShapeDtypeStruct((1, ROWS, INNER), BF16),
            jax.ShapeDtypeStruct((1, ROWS, C), BF16),
            jax.ShapeDtypeStruct((5, LETTERS, C), F32),
            jax.ShapeDtypeStruct((C,), F32),
        ),
        in_specs=[hbm] * 7,
        out_specs=(vmem, vmem, vmem, vmem),
        scratch_shapes=[
            pltpu.VMEM((1, SPAN), jnp.int32),
            pltpu.VMEM((5, LETTERS, C), BF16),
            pltpu.VMEM((C,), F32),
            pltpu.VMEM((1, ROWS, INNER), BF16),
            pltpu.VMEM((3, C, INNER), BF16),
            pltpu.VMEM((128, C), BF16),
            pltpu.VMEM((SPAN, 128), BF16),
            pltpu.VMEM((CODES, SPAN), BF16),
            pltpu.VMEM((ROWS, C), F32),
            pltpu.VMEM((SPAN, C), BF16),
            pltpu.VMEM((ROWS, CODES, C), F32),
            pltpu.VMEM((2, 1, 128), jnp.int32),
            pltpu.VMEM((DEPTH, 16, 128), BF16),
            pltpu.VMEM((DEPTH, 16, 128), BF16),
            pltpu.VMEM((RING, 32, WIDE), BF16),
            pltpu.VMEM((DEPTH, 16, INNER), BF16),
            pltpu.VMEM((RING, 32, WIDE), BF16),
            pltpu.VMEM((RING, 32, 384), BF16),
            pltpu.VMEM((DEPTH, 32, WIDE), BF16),
            pltpu.VMEM((DEPTH, 32, WIDE), BF16),
            pltpu.VMEM((40, C), F32),
            pltpu.VMEM((NEAR, 16, 128), BF16),
            pltpu.VMEM((NEAR, 16, 128), BF16),
            pltpu.VMEM((FAR, 16, 128), BF16),
            pltpu.VMEM((NEAR, 16, 128), BF16),
            pltpu.SemaphoreType.REGULAR((2,)),
            dma((7,)), dma((2,)), dma((2,)),
            dma((DEPTH,)), dma((DEPTH,)), dma((RING,)), dma((RING,)), dma((DEPTH,)), dma((DEPTH,)),
            dma((RING,)), dma((RING,)), dma((RING,)), dma((RING,)), dma((DEPTH,)), dma((DEPTH,)),
            dma((3,)), dma((3,)),
        ],
        compiler_params=pltpu.CompilerParams(
            collective_id=0, has_side_effects=True, vmem_limit_bytes=48 * 2**20
        ),
        cost_estimate=pl.CostEstimate(
            flops=2_000_000_000, bytes_accessed=8_000_000, transcendentals=4_000_000
        ),
    )(
        *(pltpu.with_memory_space_constraint(a, pltpu.HBM) for a in (
        dna_bases, conv_weight, conv_bias, w_query, w_key, w_value, out_grad))
    )
    return pl.pallas_call(
        write_kernel,
        name="write_results",
        out_shape=tuple(jax.ShapeDtypeStruct(a.shape, a.dtype) for a in results),
        in_specs=[vmem] * 4,
        out_specs=(hbm,) * 4,
        scratch_shapes=[dma((4,))],
        compiler_params=pltpu.CompilerParams(vmem_limit_bytes=2**20),
    )(*results)


def solution(mesh):
    in_specs = (P("dp", "seq"), P(), P(), P(), P(), P(), P("dp", "seq", None))
    out_specs = (P("dp", "seq", None), P("dp", "seq", None), P(), P())
    return jax.shard_map(
        per_device, mesh=mesh, in_specs=in_specs, out_specs=out_specs, check_vma=False
    )
```

```python
import functools

import jax
import jax.numpy as jnp
from jax import lax
from jax.experimental import pallas as pl
from jax.experimental.pallas import tpu as pltpu
from jax.sharding import PartitionSpec as P

C = 1536
HEAD = 192
LETTERS = 5
POOL = 128
INNER = 768
ROWS = 8
SPAN = ROWS * POOL
CODES = 48
WIDE = 256
LANES = 512
DEPTH = 4
RING = 8
SEQ = DEPTH * RING
NEAR = 32
FAR = 32
GELU_A = 0.7978845608028654
GELU_B = 0.044715
NT = (((1,), (1,)), ((), ()))
MESH = pl.DeviceIdType.MESH
F32 = jnp.float32
BF16 = jnp.bfloat16


def bits(value, low, count):
    return lax.bitwise_and(lax.shift_right_logical(value, low), (1 << count) - 1)


def window_start(head):
    return 384 * (head // 2) + 128 * (head % 2)


def one_hot_rows(codes):
    width = codes.shape[1]
    wide = jnp.broadcast_to(codes, (8, width))
    letter = lax.broadcasted_iota(jnp.int32, (8, width - 256), 0)
    parts = []
    for tap in range(5):
        moved = wide if tap == 2 else pltpu.roll(wide, (2 - tap) % width, 1)
        hit = moved[:, 128 : width - 128] == letter
        if tap == 0:
            hit = jnp.logical_or(hit, letter >= LETTERS)
        parts.append(jnp.where(hit, 1.0, 0.0).astype(F32))
    parts.append(jnp.zeros_like(parts[0]))
    return jnp.concatenate(parts, axis=0)


def positions_first(rows):
    full = jnp.concatenate([rows, jnp.zeros((128 - CODES, rows.shape[1]), F32)], axis=0)
    blocks = [full[:, at : at + 128].T for at in range(0, rows.shape[1], 128)]
    return jnp.concatenate(blocks, axis=0)


def gelu_twice(x):
    square = x * x
    inner = x * (square * (GELU_A * GELU_B) + GELU_A)
    tanh = jnp.tanh(inner)
    return x + x * tanh, square, tanh


def gelu_slope_twice(x, square, tanh):
    return (1.0 + tanh) + (x - x * (tanh * tanh)) * (square * (3 * GELU_A * GELU_B) + GELU_A)


def stem_kernel(
    dna_hbm, taps_hbm, bias_hbm, wq_hbm, wk_hbm, wv_hbm, grad_hbm,
    attended_ref, pooled_ref, conv_ref, conv_bias_ref,
    dna_ref, taps_ref, bias_ref, grad_ref, weights, turned, table, hot, hot_t, pooled_sum, slope_rows, slopes, halo,
    grad_send, grad_rows, grad_all, pool_rows, k_all, qv_all, back_send, back_rows,
    acc, chunks, near_rows, far_rows, full,
    met_sem, load_sem, halo_ss, halo_rs, g1_ss, g1_rs, g2_ss, g2_rs, p_ss, p_rs, k_ss, k_rs, q_ss, q_rs, b_ss, b_rs,
    s_ss, s_rs,
):
    dp = lax.axis_index("dp")
    seq = lax.axis_index("seq")
    head, col = bits(seq, 3, 2), bits(seq, 0, 3)
    near = col * 4 + bits(dp, 0, 2)
    far = bits(dp, 2, 2) * 8 + bits(dp, 4, 1) * 4 + head

    def along_z(step):
        return (dp, lax.bitwise_and(seq + (step * RING + SEQ), SEQ - 1))

    def along_x(step):
        return (dp, head * RING + lax.bitwise_and(col + step, RING - 1))

    def along_seq(step):
        return (dp, lax.bitwise_and(seq + (step + SEQ), SEQ - 1))

    def device_at(near, far):
        return (
            bits(far, 2, 1) * 16 + bits(far, 3, 2) * 4 + bits(near, 0, 2),
            bits(far, 0, 2) * RING + bits(near, 2, 3),
        )

    def along_near(step):
        to = lax.bitwise_and(near + step, NEAR - 1)
        return to, device_at(to, far)

    def along_far(step):
        return device_at(near, lax.bitwise_and(far + step, FAR - 1))

    def remote(src, dst, ss, rs, device):
        return pltpu.make_async_remote_copy(
            src_ref=src, dst_ref=dst, send_sem=ss, recv_sem=rs, device_id=device, device_id_type=MESH
        )

    other_core = (dp + 1 - 2 * bits(dp, 0, 1), seq)
    other_y = (dp + 2 - 4 * bits(dp, 1, 1), seq)
    other_half = (dp + 16 - 32 * bits(dp, 4, 1), seq)
    quad = bits(dp, 2, 2)
    pairs_y = [(dp + 4 * (lax.bitwise_and(quad + step, 3) - quad), seq) for step in (1, 2, 3)]
    column = [along_z(step) for step in range(1, DEPTH)]
    first_met = [
        along_seq(1), along_seq(-1), *column, *(along_x(step) for step in (4, 3, 5, 2, 6, 1, 7)),
        other_half, *pairs_y, other_y, other_core,
    ]
    barrier = pltpu.get_barrier_semaphore()
    for device in first_met:
        pl.semaphore_signal(barrier, inc=1, device_id=device, device_id_type=MESH)

    def tell(at, devices):
        for device in devices:
            pl.semaphore_signal(met_sem.at[at], inc=1, device_id=device, device_id_type=MESH)

    small = ((dna_hbm, dna_ref), (taps_hbm, taps_ref), (bias_hbm, bias_ref), (grad_hbm, grad_ref))
    reads = [pltpu.make_async_copy(hbm, ref, load_sem.at[3 + i]) for i, (hbm, ref) in enumerate(small)]
    loads = [
        pltpu.make_async_copy(hbm, weights.at[i], load_sem.at[i])
        for i, hbm in enumerate((wq_hbm, wk_hbm, wv_hbm))
    ]
    for copy in (*reads, *loads):
        copy.start()

    for copy in reads:
        copy.wait()

    bias = bias_ref[...].reshape(1, C)
    bias_high = bias.astype(BF16).astype(F32)
    bias_mid = (bias - bias_high).astype(BF16).astype(F32)
    bias_low = bias - bias_high - bias_mid
    for tap in range(5):
        letters = taps_ref[tap].astype(F32)
        spare = [bias_high, bias_mid, bias_low] if tap == 0 else [jnp.zeros((3, C), F32)]
        pair = jnp.concatenate([letters, *spare], axis=0)
        acc[8 * tap : 8 * tap + 8, :] = pair
    table[0:48, :] = jnp.concatenate([acc[...], jnp.zeros((8, C), F32)], axis=0).astype(BF16)
    table[48:128, :] = jnp.zeros((80, C), BF16)

    codes = dna_ref[...]
    outside = jnp.full((1, 128), -1, jnp.int32)
    rows = one_hot_rows(jnp.concatenate([outside, codes, outside], axis=1))
    hot_t[...] = rows.astype(BF16)
    hot[...] = positions_first(rows).astype(BF16)

    def pre_act(block, lanes):
        return jnp.dot(
            hot[block * POOL : (block + 1) * POOL, :], table[:, lanes], preferred_element_type=F32
        )

    def lanes_of(part):
        return pl.ds(pl.multiple_of(part * LANES, LANES), LANES)

    def pools(blocks):
        def body(part, _):
            lanes = lanes_of(part)
            for block in blocks:
                twice, _, _ = gelu_twice(pre_act(block, lanes))
                pooled_sum[block : block + 1, lanes] = jnp.sum(twice, axis=0, keepdims=True)
            return 0

        return body

    inner, ends = pools(range(1, ROWS - 1)), pools((0, ROWS - 1))

    def slope_part(part, _):
        lanes = lanes_of(part)
        for block in range(ROWS):
            x = pre_act(block, lanes)
            _, square, tanh = gelu_twice(x)
            slope = gelu_slope_twice(x, square, tanh)
            slope_rows[block * POOL : (block + 1) * POOL, lanes] = slope.astype(BF16)
        return 0

    lane = lax.broadcasted_iota(jnp.int32, (ROWS, WIDE), 1)
    grad = grad_ref[0].astype(F32)
    for h in range(DEPTH):
        low = 64 * (h % 2)
        start = window_start(h)
        keep = jnp.logical_and(lane >= low, lane < low + HEAD)
        window = jnp.where(keep, grad[:, start : start + WIDE], 0.0)
        if h % 2 == 0:
            window = pltpu.roll(window, 64, 1)
        grad_send[h] = jnp.concatenate([window[:, :128], window[:, 128:]], axis=0).astype(BF16)

    lax.fori_loop(0, 1, inner, 0)
    pl.semaphore_wait(barrier, len(first_met))

    halo_sends = [
        remote(dna_ref.at[:, SPAN - 128 : SPAN], halo.at[0], halo_ss.at[0], halo_rs.at[0], along_seq(1)),
        remote(dna_ref.at[:, 0:128], halo.at[1], halo_ss.at[1], halo_rs.at[1], along_seq(-1)),
    ]
    for copy in halo_sends:
        copy.start()
    g1 = [
        remote(
            grad_send.at[lax.bitwise_and(head + step, DEPTH - 1)], grad_rows.at[step],
            g1_ss.at[step], g1_rs.at[step], along_z(step),
        )
        for step in range(1, DEPTH)
    ]
    for copy in g1:
        copy.start()
    grad_rows[0] = grad_send[head]
    tell(0, (other_core, other_y, other_half, *column))

    lax.fori_loop(1, C // LANES, inner, 0)

    for copy in halo_sends:
        copy.wait()
    before = jnp.where(seq == 0, -1, halo[0])
    after = jnp.where(seq == SEQ - 1, -1, halo[1])
    first = one_hot_rows(jnp.concatenate([before, codes[:, :256]], axis=1))
    last = one_hot_rows(jnp.concatenate([codes[:, SPAN - 256 :], after], axis=1))
    hot_t[:, :POOL] = first.astype(BF16)
    hot_t[:, SPAN - POOL :] = last.astype(BF16)
    hot[:POOL, :] = positions_first(first).astype(BF16)
    hot[SPAN - POOL :, :] = positions_first(last).astype(BF16)
    lax.fori_loop(0, C // LANES, ends, 0)

    pooled = pooled_sum[...] * (0.5 / POOL)
    pooled_ref[0] = pooled.astype(BF16)
    pool_rows[0] = jnp.concatenate([pooled[:, :INNER], pooled[:, INNER:]], axis=0).astype(BF16)
    p1 = [
        remote(pool_rows.at[0], pool_rows.at[step], p_ss.at[step], p_rs.at[step], along_z(step))
        for step in range(1, DEPTH)
    ]
    for copy in p1:
        copy.start()

    for copy in g1:
        copy.wait()
    blocks = grad_rows[...].astype(F32)
    grad_all[0] = jnp.concatenate(
        [jnp.concatenate([blocks[i, :8], blocks[i, 8:]], axis=1) for i in range(DEPTH)], axis=0
    ).astype(BF16)
    g2 = [
        remote(grad_all.at[0], grad_all.at[step], g2_ss.at[step], g2_rs.at[step], along_x(step))
        for step in range(1, RING)
    ]
    for copy in g2:
        copy.start()

    lax.fori_loop(0, C // LANES - 1, slope_part, 0)

    for load in loads:
        load.wait()
    for copy in p1:
        copy.wait()
    pl.semaphore_wait(met_sem.at[0], 6)
    tell(1, (other_core, other_half))
    odd = bits(head, 0, 1)
    start = pl.multiple_of(384 * bits(head, 1, 1) + 128 * odd, 128)
    low = 64 * odd
    lane = lax.broadcasted_iota(jnp.int32, (4 * ROWS, WIDE), 1)
    keep = jnp.logical_and(lane >= low, lane < low + HEAD)
    halves = pool_rows[...].reshape(DEPTH * 16, INNER)

    def projected(i):
        left = jnp.dot(halves, weights[i, :INNER, pl.ds(start, WIDE)], preferred_element_type=F32)
        right = jnp.dot(halves, weights[i, INNER:, pl.ds(start, WIDE)], preferred_element_type=F32)
        rows = jnp.concatenate(
            [left[16 * j : 16 * j + 8] + right[16 * j + 8 : 16 * j + 16] for j in range(DEPTH)], axis=0
        )
        return pltpu.roll(jnp.where(keep, rows, 0.0), 192 * odd, 1)

    def round_x(ref, ss, rs):
        copies = [
            remote(ref.at[0], ref.at[step], ss.at[step], rs.at[step], along_x(step))
            for step in (4, 3, 5, 2, 6, 1, 7)
        ]
        for copy in copies:
            copy.start()
        return copies

    key = projected(1)
    key_tail = key[:16, 128:] + pltpu.roll(key[16:, 128:], 64, 1)
    k_all[0] = jnp.concatenate([key[:, :128], key_tail], axis=0).astype(BF16)
    k1 = round_x(k_all, k_ss, k_rs)
    query, value = projected(0), pltpu.roll(projected(2), 64, 1)
    qv_all[0] = jnp.concatenate(
        [query[:, :128], query[:, 128:] + value[:, :128], value[:, 128:]], axis=1
    ).astype(BF16)
    q1 = round_x(qv_all, q_ss, q_rs) + k1
    lax.fori_loop(C // LANES - 1, C // LANES, slope_part, 0)
    for block in range(ROWS):
        rows = slice(block * POOL, (block + 1) * POOL)
        slopes[block] = jnp.dot(hot_t[:, rows], slope_rows[rows, :], preferred_element_type=F32)
    def turn(part, _):
        rows = pl.ds(pl.multiple_of(part * 128, 128), 128)
        for i in range(3):
            turned[i, :, rows] = weights[i, rows, :].T
        return 0

    lax.fori_loop(0, C // 128, turn, 0)
    for copy in g2:
        copy.wait()
    for copy in q1:
        copy.wait()

    everyone = RING * 32
    q = qv_all[:, :, :WIDE].reshape(everyone, WIDE)
    v = qv_all[:, :, 128:].reshape(everyone, WIDE)
    tails = k_all[:, 32:48, :].astype(F32)
    low_lanes = lax.broadcasted_iota(jnp.int32, tails.shape, 2) < 64
    first_tail = jnp.where(low_lanes, tails, 0.0)
    last_tail = jnp.where(low_lanes, pltpu.roll(tails, 64, 2), 0.0)
    key_tail = jnp.concatenate([first_tail, last_tail], axis=1).astype(BF16)
    k = jnp.concatenate([k_all[:, :32, :], key_tail], axis=2).reshape(everyone, WIDE)
    g = grad_all[...].reshape(everyone, WIDE)
    scale = HEAD ** (-0.5)

    def soft_parts(scores, d_soft, axis):
        scores = scores * scale
        shifted = jnp.exp(scores - jnp.max(scores, axis=axis, keepdims=True))
        soft = shifted / jnp.sum(shifted, axis=axis, keepdims=True)
        delta = jnp.sum(soft * d_soft, axis=axis, keepdims=True)
        return soft, delta

    def finish(soft, d_soft, delta):
        return soft.astype(BF16), (soft * (d_soft - delta) * scale).astype(BF16)

    scores_t = lax.dot_general(k, q, NT, preferred_element_type=F32)
    d_soft_t = lax.dot_general(v, g, NT, preferred_element_type=F32)
    scores_own = lax.dot_general(q[:32], k, NT, preferred_element_type=F32)
    d_soft_own = lax.dot_general(g[:32], v, NT, preferred_element_type=F32)
    soft_t, delta_t = soft_parts(scores_t, d_soft_t, 0)
    half_t, d_half_t = finish(soft_t[:32], d_soft_t[:32], delta_t)
    soft_own, delta_own = soft_parts(scores_own, d_soft_own, 1)
    half_own, d_half_own = finish(soft_own, d_soft_own, delta_own)
    results = (
        jnp.dot(half_own, v, preferred_element_type=F32),
        jnp.dot(d_half_own, k, preferred_element_type=F32),
        jnp.dot(d_half_t, q, preferred_element_type=F32),
        jnp.dot(half_t, g, preferred_element_type=F32),
    )
    low_side, high_side = 64 * odd, 192 * (1 - odd)
    results = (
        pltpu.roll(jnp.where(lane >= 64, results[0], 0.0), high_side, 1),
        pltpu.roll(results[1], low_side, 1),
        pltpu.roll(jnp.where(lane < HEAD, results[2], 0.0), low_side, 1),
        pltpu.roll(results[3], high_side, 1),
    )
    for i in range(DEPTH):
        mine = jnp.concatenate([result[8 * i : 8 * i + 8] for result in results], axis=0).astype(BF16)
        if i == 0:
            back_rows[0] = mine
        else:
            back_send[i] = mine
    b1 = [
        remote(back_send.at[i], back_rows.at[i], b_ss.at[i], b_rs.at[i], along_z(-i))
        for i in range(1, DEPTH)
    ]
    for copy in b1:
        copy.start()
    for copy in b1:
        copy.wait()

    by_head = [back_rows[lax.bitwise_and(h - head + DEPTH, DEPTH - 1)].astype(F32) for h in range(DEPTH)]

    def joined(i):
        a, b, c, d = (rows[8 * i : 8 * i + 8] for rows in by_head)
        return jnp.concatenate(
            [a[:, :128], a[:, 128:] + b[:, :128], b[:, 128:], c[:, :128], c[:, 128:] + d[:, :128], d[:, 128:]],
            axis=1,
        ).astype(BF16)

    attended_ref[0] = joined(0)
    d_pooled = jnp.dot(joined(1), turned[0], preferred_element_type=F32)
    d_pooled += jnp.dot(joined(2), turned[1], preferred_element_type=F32)
    d_pooled += jnp.dot(joined(3), turned[2], preferred_element_type=F32)
    d_pooled *= 0.5 / POOL
    total = slopes[0, 0:40, :] * d_pooled[0:1]
    for block in range(1, ROWS):
        total += slopes[block, 0:40, :] * d_pooled[block : block + 1]
    for tap in range(5):
        for part in range(6):
            rows, at = slice(8 * tap, 8 * tap + 8), 256 * part
            chunk = [total[rows, at : at + 128], total[rows, at + 128 : at + 256]]
            chunks[6 * tap + part] = jnp.concatenate(chunk, axis=0).astype(BF16)
    chunks[30:32] = jnp.zeros((2, 16, 128), BF16)

    def outward(turn, centre):
        side = bits(turn, 0, 1)
        return lax.bitwise_and(centre + (1 - 2 * side) * bits(turn + 1, 1, 5), 31)

    def scatter(turn, _):
        step = outward(turn, 16)
        to, device = along_near(step)
        remote(chunks.at[to], near_rows.at[step], s_ss.at[0], s_rs.at[0], device).start()
        return 0

    def spread(turn, _):
        step = outward(turn, 20)
        remote(far_rows.at[0], far_rows.at[step], s_ss.at[1], s_rs.at[1], along_far(step)).start()
        return 0

    def gather(turn, _):
        mine = full.at[near]
        remote(mine, mine, s_ss.at[2], s_rs.at[2], along_near(outward(turn, 16))[1]).start()
        return 0

    def wait_all(ref, at):
        remote(ref, ref, s_ss.at[at], s_rs.at[at], along_z(1)).wait()

    pl.semaphore_wait(met_sem.at[1], 2)
    lax.fori_loop(0, NEAR - 1, scatter, 0)
    wait_all(near_rows.at[1:NEAR], 0)
    near_sum = chunks[near].astype(F32) + jnp.sum(near_rows[1:NEAR].astype(F32), axis=0)
    far_rows[0] = near_sum.astype(BF16)
    lax.fori_loop(0, 24, spread, 0)
    lax.fori_loop(25, FAR, spread, 0)
    wait_all(far_rows.at[1:FAR], 1)
    far_sum = far_rows[far].astype(F32)
    for i in range(1, FAR):
        far_sum += far_rows[lax.bitwise_and(far + (FAR - i), FAR - 1)].astype(F32)
    full[near] = far_sum.astype(BF16)
    lax.fori_loop(0, NEAR - 1, gather, 0)
    wait_all(full.at[0 : NEAR - 1], 2)
    for tap in range(5):
        for part in range(6):
            chunk = full[6 * tap + part].astype(F32)
            for side in range(2):
                lanes = slice(256 * part + 128 * side, 256 * part + 128 * side + 128)
                conv_ref[tap, :, lanes] = chunk[8 * side : 8 * side + LETTERS]
                if tap == 0:
                    conv_bias_ref[lanes] = chunk[8 * side + LETTERS]


def write_kernel(*refs):
    count = len(refs) // 2
    sems = refs[-1]
    copies = [pltpu.make_async_copy(refs[i], refs[count + i], sems.at[i]) for i in range(count)]
    for copy in copies:
        copy.start()
    for copy in copies:
        copy.wait()


def per_device(dna_bases, conv_weight, conv_bias, w_query, w_key, w_value, out_grad):
    vmem = pl.BlockSpec(memory_space=pltpu.VMEM)
    hbm = pl.BlockSpec(memory_space=pltpu.HBM)
    dma = pltpu.SemaphoreType.DMA
    results = pl.pallas_call(
        stem_kernel,
        name="genomic_stem",
        out_shape=(
            jax.ShapeDtypeStruct((1, ROWS, INNER), BF16),
            jax.ShapeDtypeStruct((1, ROWS, C), BF16),
            jax.ShapeDtypeStruct((5, LETTERS, C), F32),
            jax.ShapeDtypeStruct((C,), F32),
        ),
        in_specs=[hbm] * 7,
        out_specs=(vmem, vmem, vmem, vmem),
        scratch_shapes=[
            pltpu.VMEM((1, SPAN), jnp.int32),
            pltpu.VMEM((5, LETTERS, C), BF16),
            pltpu.VMEM((C,), F32),
            pltpu.VMEM((1, ROWS, INNER), BF16),
            pltpu.VMEM((3, C, INNER), BF16),
            pltpu.VMEM((3, INNER, C), BF16),
            pltpu.VMEM((128, C), BF16),
            pltpu.VMEM((SPAN, 128), BF16),
            pltpu.VMEM((CODES, SPAN), BF16),
            pltpu.VMEM((ROWS, C), F32),
            pltpu.VMEM((SPAN, C), BF16),
            pltpu.VMEM((ROWS, CODES, C), F32),
            pltpu.VMEM((2, 1, 128), jnp.int32),
            pltpu.VMEM((DEPTH, 16, 128), BF16),
            pltpu.VMEM((DEPTH, 16, 128), BF16),
            pltpu.VMEM((RING, 32, WIDE), BF16),
            pltpu.VMEM((DEPTH, 16, INNER), BF16),
            pltpu.VMEM((RING, 48, 128), BF16),
            pltpu.VMEM((RING, 32, 384), BF16),
            pltpu.VMEM((DEPTH, 32, WIDE), BF16),
            pltpu.VMEM((DEPTH, 32, WIDE), BF16),
            pltpu.VMEM((40, C), F32),
            pltpu.VMEM((NEAR, 16, 128), BF16),
            pltpu.VMEM((NEAR, 16, 128), BF16),
            pltpu.VMEM((FAR, 16, 128), BF16),
            pltpu.VMEM((NEAR, 16, 128), BF16),
            pltpu.SemaphoreType.REGULAR((2,)),
            dma((7,)), dma((2,)), dma((2,)),
            dma((DEPTH,)), dma((DEPTH,)), dma((RING,)), dma((RING,)), dma((DEPTH,)), dma((DEPTH,)),
            dma((RING,)), dma((RING,)), dma((RING,)), dma((RING,)), dma((DEPTH,)), dma((DEPTH,)),
            dma((3,)), dma((3,)),
        ],
        compiler_params=pltpu.CompilerParams(
            collective_id=0, has_side_effects=True, vmem_limit_bytes=48 * 2**20
        ),
        cost_estimate=pl.CostEstimate(
            flops=2_000_000_000, bytes_accessed=8_000_000, transcendentals=4_000_000
        ),
    )(
        *(pltpu.with_memory_space_constraint(a, pltpu.HBM) for a in (
        dna_bases, conv_weight, conv_bias, w_query, w_key, w_value, out_grad))
    )
    return pl.pallas_call(
        write_kernel,
        name="write_results",
        out_shape=tuple(jax.ShapeDtypeStruct(a.shape, a.dtype) for a in results),
        in_specs=[vmem] * 4,
        out_specs=(hbm,) * 4,
        scratch_shapes=[dma((4,))],
        compiler_params=pltpu.CompilerParams(vmem_limit_bytes=2**20),
    )(*results)


def solution(mesh):
    in_specs = (P("dp", "seq"), P(), P(), P(), P(), P(), P("dp", "seq", None))
    out_specs = (P("dp", "seq", None), P("dp", "seq", None), P(), P())
    return jax.shard_map(
        per_device, mesh=mesh, in_specs=in_specs, out_specs=out_specs, check_vma=False
    )
```

```python
import functools

import jax
import jax.numpy as jnp
from jax import lax
from jax.experimental import pallas as pl
from jax.experimental.pallas import tpu as pltpu
from jax.sharding import PartitionSpec as P

C = 1536
HEAD = 192
LETTERS = 5
POOL = 128
INNER = 768
ROWS = 8
SPAN = ROWS * POOL
CODES = 48
WIDE = 256
LANES = 512
DEPTH = 4
RING = 8
SEQ = DEPTH * RING
NEAR = 32
FAR = 32
GELU_A = 0.7978845608028654
GELU_B = 0.044715
NT = (((1,), (1,)), ((), ()))
MESH = pl.DeviceIdType.MESH
F32 = jnp.float32
BF16 = jnp.bfloat16


def bits(value, low, count):
    return lax.bitwise_and(lax.shift_right_logical(value, low), (1 << count) - 1)


def window_start(head):
    return 384 * (head // 2) + 128 * (head % 2)


def one_hot_rows(codes):
    width = codes.shape[1]
    wide = jnp.broadcast_to(codes, (8, width))
    letter = lax.broadcasted_iota(jnp.int32, (8, width - 256), 0)
    parts = []
    for tap in range(5):
        moved = wide if tap == 2 else pltpu.roll(wide, (2 - tap) % width, 1)
        hit = moved[:, 128 : width - 128] == letter
        if tap == 0:
            hit = jnp.logical_or(hit, letter >= LETTERS)
        parts.append(jnp.where(hit, 1.0, 0.0).astype(F32))
    parts.append(jnp.zeros_like(parts[0]))
    return jnp.concatenate(parts, axis=0)


def positions_first(rows):
    full = jnp.concatenate([rows, jnp.zeros((128 - CODES, rows.shape[1]), F32)], axis=0)
    blocks = [full[:, at : at + 128].T for at in range(0, rows.shape[1], 128)]
    return jnp.concatenate(blocks, axis=0)


def gelu_twice(x):
    square = x * x
    inner = x * (square * (GELU_A * GELU_B) + GELU_A)
    tanh = jnp.tanh(inner)
    return x + x * tanh, square, tanh


def gelu_slope_twice(x, square, tanh):
    return (1.0 + tanh) + (x - x * (tanh * tanh)) * (square * (3 * GELU_A * GELU_B) + GELU_A)


def stem_kernel(
    dna_hbm, taps_hbm, bias_hbm, wq_hbm, wk_hbm, wv_hbm, grad_hbm,
    attended_ref, pooled_ref, conv_ref, conv_bias_ref,
    dna_ref, taps_ref, bias_ref, grad_ref, weights, turned, table, hot, hot_t, pooled_sum, slope_rows, slopes, ends,
    grad_send, grad_rows, grad_all, pool_rows, k_all, qv_all, back_send, back_rows,
    acc, chunks, near_rows, far_rows, full,
    met_sem, load_sem, end_ss, end_rs, g1_ss, g1_rs, g2_ss, g2_rs, p_ss, p_rs, k_ss, k_rs, q_ss, q_rs, b_ss, b_rs,
    s_ss, s_rs,
):
    dp = lax.axis_index("dp")
    seq = lax.axis_index("seq")
    head, col = bits(seq, 3, 2), bits(seq, 0, 3)
    near = col * 4 + bits(dp, 0, 2)
    far = bits(dp, 2, 2) * 8 + bits(dp, 4, 1) * 4 + head

    def along_z(step):
        return (dp, lax.bitwise_and(seq + (step * RING + SEQ), SEQ - 1))

    def along_x(step):
        return (dp, head * RING + lax.bitwise_and(col + step, RING - 1))

    def beside(side, step):
        return (
            dp,
            lax.bitwise_and(head + step, DEPTH - 1) * RING + lax.bitwise_and(col + (side + RING), RING - 1),
        )

    def device_at(near, far):
        return (
            bits(far, 2, 1) * 16 + bits(far, 3, 2) * 4 + bits(near, 0, 2),
            bits(far, 0, 2) * RING + bits(near, 2, 3),
        )

    def along_near(step):
        to = lax.bitwise_and(near + step, NEAR - 1)
        return to, device_at(to, far)

    def along_far(step):
        return device_at(near, lax.bitwise_and(far + step, FAR - 1))

    def remote(src, dst, ss, rs, device):
        return pltpu.make_async_remote_copy(
            src_ref=src, dst_ref=dst, send_sem=ss, recv_sem=rs, device_id=device, device_id_type=MESH
        )

    other_core = (dp + 1 - 2 * bits(dp, 0, 1), seq)
    other_y = (dp + 2 - 4 * bits(dp, 1, 1), seq)
    other_half = (dp + 16 - 32 * bits(dp, 4, 1), seq)
    quad = bits(dp, 2, 2)
    pairs_y = [(dp + 4 * (lax.bitwise_and(quad + step, 3) - quad), seq) for step in (1, 2, 3)]
    column = [along_z(step) for step in range(1, DEPTH)]
    first_met = [
        *(beside(side, step) for side in (1, -1) for step in (2, 1, 3)), *column, *(along_x(step) for step in (4, 3, 5, 2, 6, 1, 7)),
        other_half, *pairs_y, other_y, other_core,
    ]
    barrier = pltpu.get_barrier_semaphore()
    for device in first_met:
        pl.semaphore_signal(barrier, inc=1, device_id=device, device_id_type=MESH)

    def tell(at, devices):
        for device in devices:
            pl.semaphore_signal(met_sem.at[at], inc=1, device_id=device, device_id_type=MESH)

    small = ((dna_hbm, dna_ref), (taps_hbm, taps_ref), (bias_hbm, bias_ref), (grad_hbm, grad_ref))
    reads = [pltpu.make_async_copy(hbm, ref, load_sem.at[3 + i]) for i, (hbm, ref) in enumerate(small)]
    loads = [
        pltpu.make_async_copy(hbm, weights.at[i], load_sem.at[i])
        for i, hbm in enumerate((wq_hbm, wk_hbm, wv_hbm))
    ]
    for copy in (*reads, *loads):
        copy.start()

    for copy in reads:
        copy.wait()

    bias = bias_ref[...].reshape(1, C)
    bias_high = bias.astype(BF16).astype(F32)
    bias_mid = (bias - bias_high).astype(BF16).astype(F32)
    bias_low = bias - bias_high - bias_mid
    for tap in range(5):
        letters = taps_ref[tap].astype(F32)
        spare = [bias_high, bias_mid, bias_low] if tap == 0 else [jnp.zeros((3, C), F32)]
        pair = jnp.concatenate([letters, *spare], axis=0)
        acc[8 * tap : 8 * tap + 8, :] = pair
    table[0:48, :] = jnp.concatenate([acc[...], jnp.zeros((8, C), F32)], axis=0).astype(BF16)
    table[48:128, :] = jnp.zeros((80, C), BF16)

    codes = dna_ref[...]
    outside = jnp.full((1, 128), -1, jnp.int32)
    rows = one_hot_rows(jnp.concatenate([outside, codes, outside], axis=1))
    hot_t[...] = rows.astype(BF16)
    hot[...] = positions_first(rows).astype(BF16)

    def pre_act(block, lanes):
        return jnp.dot(
            hot[block * POOL : (block + 1) * POOL, :], table[:, lanes], preferred_element_type=F32
        )

    def lanes_of(part):
        return pl.ds(pl.multiple_of(part * LANES, LANES), LANES)

    row = lax.broadcasted_iota(jnp.int32, (POOL, LANES), 0)

    def pools(part, _):
        lanes = lanes_of(part)
        for block in range(ROWS):
            twice, _, _ = gelu_twice(pre_act(block, lanes))
            if block == 0:
                twice = jnp.where(row >= 2, twice, 0.0)
            if block == ROWS - 1:
                twice = jnp.where(row < POOL - 2, twice, 0.0)
            pooled_sum[block : block + 1, lanes] = jnp.sum(twice, axis=0, keepdims=True)
        return 0

    def slope_part(part, _):
        lanes = lanes_of(part)
        for block in range(ROWS):
            x = pre_act(block, lanes)
            _, square, tanh = gelu_twice(x)
            slope = gelu_slope_twice(x, square, tanh)
            slope_rows[block * POOL : (block + 1) * POOL, lanes] = slope.astype(BF16)
        return 0

    lane = lax.broadcasted_iota(jnp.int32, (ROWS, WIDE), 1)
    grad = grad_ref[0].astype(F32)
    for h in range(DEPTH):
        low = 64 * (h % 2)
        start = window_start(h)
        keep = jnp.logical_and(lane >= low, lane < low + HEAD)
        window = jnp.where(keep, grad[:, start : start + WIDE], 0.0)
        if h % 2 == 0:
            window = pltpu.roll(window, 64, 1)
        grad_send[h] = jnp.concatenate([window[:, :128], window[:, 128:]], axis=0).astype(BF16)

    ends[1, 0] = jnp.concatenate([codes[:, :128], codes[:, SPAN - 128 :]], axis=1)
    lax.fori_loop(0, 1, pools, 0)
    pl.semaphore_wait(barrier, len(first_met))

    end_sends = [
        remote(
            ends.at[1, 0], ends.at[1 - side, step],
            end_ss.at[4 * (1 - side) + step], end_rs.at[4 * (1 - side) + step], beside(side, step),
        )
        for side, step in ((1, 2), (-1, 2), (1, 3), (-1, 3), (1, 1), (-1, 1), (1, 0), (-1, 0), (0, 2), (0, 1), (0, 3))
    ]
    for copy in end_sends:
        copy.start()
    g1 = [
        remote(
            grad_send.at[lax.bitwise_and(head + step, DEPTH - 1)], grad_rows.at[step],
            g1_ss.at[step], g1_rs.at[step], along_z(step),
        )
        for step in range(1, DEPTH)
    ]
    for copy in g1:
        copy.start()
    grad_rows[0] = grad_send[head]
    tell(0, (other_core, other_y, other_half, *column))

    lax.fori_loop(1, C // LANES, pools, 0)

    partial = pooled_sum[...] * (0.5 / POOL)
    rest = partial - partial.astype(BF16).astype(F32)
    spare = [jnp.zeros((2, 256), F32)]
    rests = [
        jnp.concatenate([rest[at : at + 1, 256 * i : 256 * i + 256] for i in range(6)] + spare, axis=0)
        for at in (0, ROWS - 1)
    ]
    pool_rows[0] = jnp.concatenate(
        [jnp.concatenate([partial[:, :INNER], partial[:, INNER:]], axis=0), jnp.concatenate(rests, axis=0)],
        axis=1,
    ).astype(BF16)
    p1 = [
        remote(pool_rows.at[0], pool_rows.at[step], p_ss.at[step], p_rs.at[step], along_z(step))
        for step in range(1, DEPTH)
    ]
    for copy in p1:
        copy.start()

    for copy in g1:
        copy.wait()
    blocks = grad_rows[...].astype(F32)
    grad_all[0] = jnp.concatenate(
        [jnp.concatenate([blocks[i, :8], blocks[i, 8:]], axis=1) for i in range(DEPTH)], axis=0
    ).astype(BF16)
    g2 = [
        remote(grad_all.at[0], grad_all.at[step], g2_ss.at[step], g2_rs.at[step], along_x(step))
        for step in range(1, RING)
    ]
    for copy in g2:
        copy.start()

    def turn(part, _):
        rows = pl.ds(pl.multiple_of(part * 128, 128), 128)
        for i in range(3):
            turned[i, :, rows] = weights[i, rows, :].T
        return 0

    for load in loads:
        load.wait()
    lax.fori_loop(0, C // 128, turn, 0)

    for copy in end_sends:
        copy.wait()
    lane = lax.broadcasted_iota(jnp.int32, (8, 128), 1)
    line = jnp.full((8, 128), -1, jnp.int32)
    sides = []
    for i in range(DEPTH):
        level = lax.bitwise_and(head - i + DEPTH, DEPTH - 1)
        before = jnp.where(level == 0, -1, ends[0, (i + 1) % DEPTH, :, 128:])
        before = jnp.where(col == 0, before, ends[0, i, :, 128:])
        after = jnp.where(level == DEPTH - 1, -1, ends[2, (i + 3) % DEPTH, :, :128])
        after = jnp.where(col == RING - 1, after, ends[2, i, :, :128])
        sides.append((before, after))
        for at, move, source in (
            (0, 2, before), (2, 2, ends[1, i, :, :128]), (8, 12, ends[1, i, :, 128:]), (12, 12, after),
        ):
            moved = pltpu.roll(jnp.broadcast_to(source, (8, 128)), 16 * i + move, 1)
            line = jnp.where(lane >= 16 * i + at, moved, line)
    line = jnp.where(lane < 16 * DEPTH, line, -1)[:1]
    near_ends = one_hot_rows(jnp.concatenate([outside, line, outside], axis=1))
    near_ends = positions_first(near_ends)[: 16 * DEPTH].astype(BF16)
    twice, _, _ = gelu_twice(jnp.dot(near_ends, table[...], preferred_element_type=F32))
    twice = twice.reshape(2 * DEPTH, 8, C)
    place = lax.broadcasted_iota(jnp.int32, twice.shape, 1)
    twice = jnp.where(jnp.logical_or(place == 2, place == 3), twice, 0.0)
    end_parts = jnp.sum(twice, axis=1) * (0.5 / POOL)

    before, after = sides[0]
    first = one_hot_rows(jnp.concatenate([before, codes[:, :256]], axis=1))
    last = one_hot_rows(jnp.concatenate([codes[:, SPAN - 256 :], after], axis=1))
    hot_t[:, :POOL] = first.astype(BF16)
    hot_t[:, SPAN - POOL :] = last.astype(BF16)
    hot[:POOL, :] = positions_first(first).astype(BF16)
    hot[SPAN - POOL :, :] = positions_first(last).astype(BF16)

    for copy in p1:
        copy.wait()
    pl.semaphore_wait(met_sem.at[0], 6)
    tell(1, (other_core, other_half))
    odd = bits(head, 0, 1)
    start = pl.multiple_of(384 * bits(head, 1, 1) + 128 * odd, 128)
    low = 64 * odd
    lane = lax.broadcasted_iota(jnp.int32, (4 * ROWS, WIDE), 1)
    keep = jnp.logical_and(lane >= low, lane < low + HEAD)
    place = lax.broadcasted_iota(jnp.int32, (ROWS, C), 0)
    column_rows = []
    for i in range(DEPTH):
        sent = pool_rows[i].astype(F32)
        wide = jnp.concatenate([sent[:8, :INNER], sent[8:, :INNER]], axis=1)
        firsts = jnp.concatenate([sent[j : j + 1, INNER:] for j in range(6)], axis=1)
        lasts = jnp.concatenate([sent[8 + j : 9 + j, INNER:] for j in range(6)], axis=1)
        firsts += end_parts[2 * i : 2 * i + 1]
        lasts += end_parts[2 * i + 1 : 2 * i + 2]
        wide += jnp.where(place == 0, firsts, jnp.where(place == ROWS - 1, lasts, 0.0))
        column_rows.append(wide)
    column_rows = jnp.concatenate(column_rows, axis=0).astype(BF16)
    pooled_ref[0] = column_rows[:ROWS]

    def projected(i):
        rows = jnp.dot(column_rows, weights[i, :, pl.ds(start, WIDE)], preferred_element_type=F32)
        return pltpu.roll(jnp.where(keep, rows, 0.0), 192 * odd, 1)

    def round_x(ref, ss, rs):
        copies = [
            remote(ref.at[0], ref.at[step], ss.at[step], rs.at[step], along_x(step))
            for step in (4, 3, 5, 2, 6, 1, 7)
        ]
        for copy in copies:
            copy.start()
        return copies

    key = projected(1)
    key_tail = key[:16, 128:] + pltpu.roll(key[16:, 128:], 64, 1)
    k_all[0] = jnp.concatenate([key[:, :128], key_tail], axis=0).astype(BF16)
    k1 = round_x(k_all, k_ss, k_rs)
    query, value = projected(0), pltpu.roll(projected(2), 64, 1)
    qv_all[0] = jnp.concatenate(
        [query[:, :128], query[:, 128:] + value[:, :128], value[:, 128:]], axis=1
    ).astype(BF16)
    q1 = round_x(qv_all, q_ss, q_rs) + k1
    lax.fori_loop(0, C // LANES, slope_part, 0)
    for block in range(ROWS):
        rows = slice(block * POOL, (block + 1) * POOL)
        slopes[block] = jnp.dot(hot_t[:, rows], slope_rows[rows, :], preferred_element_type=F32)
    for copy in g2:
        copy.wait()
    for copy in q1:
        copy.wait()

    everyone = RING * 32
    q = qv_all[:, :, :WIDE].reshape(everyone, WIDE)
    v = qv_all[:, :, 128:].reshape(everyone, WIDE)
    tails = k_all[:, 32:48, :].astype(F32)
    low_lanes = lax.broadcasted_iota(jnp.int32, tails.shape, 2) < 64
    first_tail = jnp.where(low_lanes, tails, 0.0)
    last_tail = jnp.where(low_lanes, pltpu.roll(tails, 64, 2), 0.0)
    key_tail = jnp.concatenate([first_tail, last_tail], axis=1).astype(BF16)
    k = jnp.concatenate([k_all[:, :32, :], key_tail], axis=2).reshape(everyone, WIDE)
    g = grad_all[...].reshape(everyone, WIDE)
    scale = HEAD ** (-0.5)

    def soft_parts(scores, d_soft, axis):
        scores = scores * scale
        shifted = jnp.exp(scores - jnp.max(scores, axis=axis, keepdims=True))
        soft = shifted / jnp.sum(shifted, axis=axis, keepdims=True)
        delta = jnp.sum(soft * d_soft, axis=axis, keepdims=True)
        return soft, delta

    def finish(soft, d_soft, delta):
        return soft.astype(BF16), (soft * (d_soft - delta) * scale).astype(BF16)

    scores_t = lax.dot_general(k, q, NT, preferred_element_type=F32)
    d_soft_t = lax.dot_general(v, g, NT, preferred_element_type=F32)
    scores_own = lax.dot_general(q[:32], k, NT, preferred_element_type=F32)
    d_soft_own = lax.dot_general(g[:32], v, NT, preferred_element_type=F32)
    soft_t, delta_t = soft_parts(scores_t, d_soft_t, 0)
    half_t, d_half_t = finish(soft_t[:32], d_soft_t[:32], delta_t)
    soft_own, delta_own = soft_parts(scores_own, d_soft_own, 1)
    half_own, d_half_own = finish(soft_own, d_soft_own, delta_own)
    results = (
        jnp.dot(half_own, v, preferred_element_type=F32),
        jnp.dot(d_half_own, k, preferred_element_type=F32),
        jnp.dot(d_half_t, q, preferred_element_type=F32),
        jnp.dot(half_t, g, preferred_element_type=F32),
    )
    low_side, high_side = 64 * odd, 192 * (1 - odd)
    results = (
        pltpu.roll(jnp.where(lane >= 64, results[0], 0.0), high_side, 1),
        pltpu.roll(results[1], low_side, 1),
        pltpu.roll(jnp.where(lane < HEAD, results[2], 0.0), low_side, 1),
        pltpu.roll(results[3], high_side, 1),
    )
    for i in range(DEPTH):
        mine = jnp.concatenate([result[8 * i : 8 * i + 8] for result in results], axis=0).astype(BF16)
        if i == 0:
            back_rows[0] = mine
        else:
            back_send[i] = mine
    b1 = [
        remote(back_send.at[i], back_rows.at[i], b_ss.at[i], b_rs.at[i], along_z(-i))
        for i in range(1, DEPTH)
    ]
    for copy in b1:
        copy.start()
    for copy in b1:
        copy.wait()

    by_head = [back_rows[lax.bitwise_and(h - head + DEPTH, DEPTH - 1)].astype(F32) for h in range(DEPTH)]

    def joined(i):
        a, b, c, d = (rows[8 * i : 8 * i + 8] for rows in by_head)
        return jnp.concatenate(
            [a[:, :128], a[:, 128:] + b[:, :128], b[:, 128:], c[:, :128], c[:, 128:] + d[:, :128], d[:, 128:]],
            axis=1,
        ).astype(BF16)

    attended_ref[0] = joined(0)
    d_pooled = jnp.dot(joined(1), turned[0], preferred_element_type=F32)
    d_pooled += jnp.dot(joined(2), turned[1], preferred_element_type=F32)
    d_pooled += jnp.dot(joined(3), turned[2], preferred_element_type=F32)
    d_pooled *= 0.5 / POOL
    total = slopes[0, 0:40, :] * d_pooled[0:1]
    for block in range(1, ROWS):
        total += slopes[block, 0:40, :] * d_pooled[block : block + 1]
    for tap in range(5):
        for part in range(6):
            rows, at = slice(8 * tap, 8 * tap + 8), 256 * part
            chunk = [total[rows, at : at + 128], total[rows, at + 128 : at + 256]]
            chunks[6 * tap + part] = jnp.concatenate(chunk, axis=0).astype(BF16)
    chunks[30:32] = jnp.zeros((2, 16, 128), BF16)

    def outward(turn, centre):
        side = bits(turn, 0, 1)
        return lax.bitwise_and(centre + (1 - 2 * side) * bits(turn + 1, 1, 5), 31)

    def scatter(turn, _):
        step = outward(turn, 16)
        to, device = along_near(step)
        remote(chunks.at[to], near_rows.at[step], s_ss.at[0], s_rs.at[0], device).start()
        return 0

    def spread(turn, _):
        step = outward(turn, 20)
        remote(far_rows.at[0], far_rows.at[step], s_ss.at[1], s_rs.at[1], along_far(step)).start()
        return 0

    def gather(turn, _):
        mine = full.at[near]
        remote(mine, mine, s_ss.at[2], s_rs.at[2], along_near(outward(turn, 16))[1]).start()
        return 0

    def wait_all(ref, at):
        remote(ref, ref, s_ss.at[at], s_rs.at[at], along_z(1)).wait()

    pl.semaphore_wait(met_sem.at[1], 2)
    lax.fori_loop(0, NEAR - 1, scatter, 0)
    wait_all(near_rows.at[1:NEAR], 0)
    near_sum = chunks[near].astype(F32) + jnp.sum(near_rows[1:NEAR].astype(F32), axis=0)
    far_rows[0] = near_sum.astype(BF16)
    lax.fori_loop(0, 24, spread, 0)
    lax.fori_loop(25, FAR, spread, 0)
    wait_all(far_rows.at[1:FAR], 1)
    far_sum = far_rows[far].astype(F32)
    for i in range(1, FAR):
        far_sum += far_rows[lax.bitwise_and(far + (FAR - i), FAR - 1)].astype(F32)
    full[near] = far_sum.astype(BF16)
    lax.fori_loop(0, NEAR - 1, gather, 0)
    wait_all(full.at[0 : NEAR - 1], 2)
    for tap in range(5):
        for part in range(6):
            chunk = full[6 * tap + part].astype(F32)
            for side in range(2):
                lanes = slice(256 * part + 128 * side, 256 * part + 128 * side + 128)
                conv_ref[tap, :, lanes] = chunk[8 * side : 8 * side + LETTERS]
                if tap == 0:
                    conv_bias_ref[lanes] = chunk[8 * side + LETTERS]


def write_kernel(*refs):
    count = len(refs) // 2
    sems = refs[-1]
    copies = [pltpu.make_async_copy(refs[i], refs[count + i], sems.at[i]) for i in range(count)]
    for copy in copies:
        copy.start()
    for copy in copies:
        copy.wait()


def per_device(dna_bases, conv_weight, conv_bias, w_query, w_key, w_value, out_grad):
    vmem = pl.BlockSpec(memory_space=pltpu.VMEM)
    hbm = pl.BlockSpec(memory_space=pltpu.HBM)
    dma = pltpu.SemaphoreType.DMA
    results = pl.pallas_call(
        stem_kernel,
        name="genomic_stem",
        out_shape=(
            jax.ShapeDtypeStruct((1, ROWS, INNER), BF16),
            jax.ShapeDtypeStruct((1, ROWS, C), BF16),
            jax.ShapeDtypeStruct((5, LETTERS, C), F32),
            jax.ShapeDtypeStruct((C,), F32),
        ),
        in_specs=[hbm] * 7,
        out_specs=(vmem, vmem, vmem, vmem),
        scratch_shapes=[
            pltpu.VMEM((1, SPAN), jnp.int32),
            pltpu.VMEM((5, LETTERS, C), BF16),
            pltpu.VMEM((C,), F32),
            pltpu.VMEM((1, ROWS, INNER), BF16),
            pltpu.VMEM((3, C, INNER), BF16),
            pltpu.VMEM((3, INNER, C), BF16),
            pltpu.VMEM((128, C), BF16),
            pltpu.VMEM((SPAN, 128), BF16),
            pltpu.VMEM((CODES, SPAN), BF16),
            pltpu.VMEM((ROWS, C), F32),
            pltpu.VMEM((SPAN, C), BF16),
            pltpu.VMEM((ROWS, CODES, C), F32),
            pltpu.VMEM((3, DEPTH, 1, 256), jnp.int32),
            pltpu.VMEM((DEPTH, 16, 128), BF16),
            pltpu.VMEM((DEPTH, 16, 128), BF16),
            pltpu.VMEM((RING, 32, WIDE), BF16),
            pltpu.VMEM((DEPTH, 16, INNER + 256), BF16),
            pltpu.VMEM((RING, 48, 128), BF16),
            pltpu.VMEM((RING, 32, 384), BF16),
            pltpu.VMEM((DEPTH, 32, WIDE), BF16),
            pltpu.VMEM((DEPTH, 32, WIDE), BF16),
            pltpu.VMEM((40, C), F32),
            pltpu.VMEM((NEAR, 16, 128), BF16),
            pltpu.VMEM((NEAR, 16, 128), BF16),
            pltpu.VMEM((FAR, 16, 128), BF16),
            pltpu.VMEM((NEAR, 16, 128), BF16),
            pltpu.SemaphoreType.REGULAR((2,)),
            dma((7,)), dma((12,)), dma((12,)),
            dma((DEPTH,)), dma((DEPTH,)), dma((RING,)), dma((RING,)), dma((DEPTH,)), dma((DEPTH,)),
            dma((RING,)), dma((RING,)), dma((RING,)), dma((RING,)), dma((DEPTH,)), dma((DEPTH,)),
            dma((3,)), dma((3,)),
        ],
        compiler_params=pltpu.CompilerParams(
            collective_id=0, has_side_effects=True, vmem_limit_bytes=48 * 2**20
        ),
        cost_estimate=pl.CostEstimate(
            flops=2_000_000_000, bytes_accessed=8_000_000, transcendentals=4_000_000
        ),
    )(
        *(pltpu.with_memory_space_constraint(a, pltpu.HBM) for a in (
        dna_bases, conv_weight, conv_bias, w_query, w_key, w_value, out_grad))
    )
    return pl.pallas_call(
        write_kernel,
        name="write_results",
        out_shape=tuple(jax.ShapeDtypeStruct(a.shape, a.dtype) for a in results),
        in_specs=[vmem] * 4,
        out_specs=(hbm,) * 4,
        scratch_shapes=[dma((4,))],
        compiler_params=pltpu.CompilerParams(vmem_limit_bytes=2**20),
    )(*results)


def solution(mesh):
    in_specs = (P("dp", "seq"), P(), P(), P(), P(), P(), P("dp", "seq", None))
    out_specs = (P("dp", "seq", None), P("dp", "seq", None), P(), P())
    return jax.shard_map(
        per_device, mesh=mesh, in_specs=in_specs, out_specs=out_specs, check_vma=False
    )
```

```python
import functools

import jax
import jax.numpy as jnp
from jax import lax
from jax.experimental import pallas as pl
from jax.experimental.pallas import tpu as pltpu
from jax.sharding import PartitionSpec as P

C = 1536
HEAD = 192
LETTERS = 5
POOL = 128
INNER = 768
ROWS = 8
SPAN = ROWS * POOL
CODES = 48
WIDE = 256
LANES = 512
DEPTH = 4
RING = 8
SEQ = DEPTH * RING
NEAR = 32
FAR = 32
GELU_A = 0.7978845608028654
GELU_B = 0.044715
NT = (((1,), (1,)), ((), ()))
MESH = pl.DeviceIdType.MESH
F32 = jnp.float32
BF16 = jnp.bfloat16


def bits(value, low, count):
    return lax.bitwise_and(lax.shift_right_logical(value, low), (1 << count) - 1)


def window_start(head):
    return 384 * (head // 2) + 128 * (head % 2)


def one_hot_rows(codes):
    width = codes.shape[1]
    wide = jnp.broadcast_to(codes, (8, width))
    letter = lax.broadcasted_iota(jnp.int32, (8, width - 256), 0)
    parts = []
    for tap in range(5):
        moved = wide if tap == 2 else pltpu.roll(wide, (2 - tap) % width, 1)
        hit = moved[:, 128 : width - 128] == letter
        if tap == 0:
            hit = jnp.logical_or(hit, letter >= LETTERS)
        parts.append(jnp.where(hit, 1.0, 0.0).astype(F32))
    parts.append(jnp.zeros_like(parts[0]))
    return jnp.concatenate(parts, axis=0)


def positions_first(rows):
    full = jnp.concatenate([rows, jnp.zeros((128 - CODES, rows.shape[1]), F32)], axis=0)
    blocks = [full[:, at : at + 128].T for at in range(0, rows.shape[1], 128)]
    return jnp.concatenate(blocks, axis=0)


def gelu_twice(x):
    square = x * x
    inner = x * (square * (GELU_A * GELU_B) + GELU_A)
    tanh = jnp.tanh(inner)
    return x + x * tanh, square, tanh


def gelu_slope_twice(x, square, tanh):
    return (1.0 + tanh) + (x - x * (tanh * tanh)) * (square * (3 * GELU_A * GELU_B) + GELU_A)


def stem_kernel(
    dna_hbm, taps_hbm, bias_hbm, wq_hbm, wk_hbm, wv_hbm, grad_hbm,
    attended_ref, pooled_ref, conv_ref, conv_bias_ref,
    dna_ref, taps_ref, bias_ref, grad_ref, weights, turned, table, hot, hot_t, pooled_sum, slope_rows, slopes, ends,
    grad_send, grad_rows, grad_all, pool_rows, k_all, qv_all, back_send, back_rows,
    acc, chunks, near_rows, far_rows, full,
    met_sem, load_sem, end_ss, end_rs, g1_ss, g1_rs, g2_ss, g2_rs, p_ss, p_rs, k_ss, k_rs, q_ss, q_rs, b_ss, b_rs,
    s_ss, s_rs,
):
    dp = lax.axis_index("dp")
    seq = lax.axis_index("seq")
    head, col = bits(seq, 3, 2), bits(seq, 0, 3)
    near = col * 4 + bits(dp, 0, 2)
    far = bits(dp, 2, 2) * 8 + bits(dp, 4, 1) * 4 + head

    def along_z(step):
        return (dp, lax.bitwise_and(seq + (step * RING + SEQ), SEQ - 1))

    def along_x(step):
        return (dp, head * RING + lax.bitwise_and(col + step, RING - 1))

    def beside(side, step):
        return (
            dp,
            lax.bitwise_and(head + step, DEPTH - 1) * RING + lax.bitwise_and(col + (side + RING), RING - 1),
        )

    def device_at(near, far):
        return (
            bits(far, 2, 1) * 16 + bits(far, 3, 2) * 4 + bits(near, 0, 2),
            bits(far, 0, 2) * RING + bits(near, 2, 3),
        )

    def along_near(step):
        to = lax.bitwise_and(near + step, NEAR - 1)
        return to, device_at(to, far)

    def along_far(step):
        return device_at(near, lax.bitwise_and(far + step, FAR - 1))

    def remote(src, dst, ss, rs, device):
        return pltpu.make_async_remote_copy(
            src_ref=src, dst_ref=dst, send_sem=ss, recv_sem=rs, device_id=device, device_id_type=MESH
        )

    other_core = (dp + 1 - 2 * bits(dp, 0, 1), seq)
    other_y = (dp + 2 - 4 * bits(dp, 1, 1), seq)
    other_half = (dp + 16 - 32 * bits(dp, 4, 1), seq)
    quad = bits(dp, 2, 2)
    pairs_y = [(dp + 4 * (lax.bitwise_and(quad + step, 3) - quad), seq) for step in (1, 2, 3)]
    column = [along_z(step) for step in range(1, DEPTH)]
    first_met = [
        *(beside(side, step) for side in (1, -1) for step in (2, 1, 3)), *column, *(along_x(step) for step in (4, 3, 5, 2, 6, 1, 7)),
        other_half, *pairs_y, other_y, other_core,
    ]
    barrier = pltpu.get_barrier_semaphore()
    for device in first_met:
        pl.semaphore_signal(barrier, inc=1, device_id=device, device_id_type=MESH)

    def tell(at, devices):
        for device in devices:
            pl.semaphore_signal(met_sem.at[at], inc=1, device_id=device, device_id_type=MESH)

    small = ((dna_hbm, dna_ref), (taps_hbm, taps_ref), (bias_hbm, bias_ref), (grad_hbm, grad_ref))
    reads = [pltpu.make_async_copy(hbm, ref, load_sem.at[3 + i]) for i, (hbm, ref) in enumerate(small)]
    loads = [
        pltpu.make_async_copy(hbm, weights.at[i], load_sem.at[i])
        for i, hbm in enumerate((wq_hbm, wk_hbm, wv_hbm))
    ]
    for copy in (*reads, *loads):
        copy.start()

    for copy in reads:
        copy.wait()

    bias = bias_ref[...].reshape(1, C)
    bias_high = bias.astype(BF16).astype(F32)
    bias_mid = (bias - bias_high).astype(BF16).astype(F32)
    bias_low = bias - bias_high - bias_mid
    for tap in range(5):
        letters = taps_ref[tap].astype(F32)
        spare = [bias_high, bias_mid, bias_low] if tap == 0 else [jnp.zeros((3, C), F32)]
        pair = jnp.concatenate([letters, *spare], axis=0)
        acc[8 * tap : 8 * tap + 8, :] = pair
    table[0:48, :] = jnp.concatenate([acc[...], jnp.zeros((8, C), F32)], axis=0).astype(BF16)
    table[48:128, :] = jnp.zeros((80, C), BF16)

    codes = dna_ref[...]
    outside = jnp.full((1, 128), -1, jnp.int32)
    rows = one_hot_rows(jnp.concatenate([outside, codes, outside], axis=1))
    hot_t[...] = rows.astype(BF16)
    hot[...] = positions_first(rows).astype(BF16)

    def pre_act(block, lanes):
        return jnp.dot(
            hot[block * POOL : (block + 1) * POOL, :], table[:, lanes], preferred_element_type=F32
        )

    def lanes_of(part):
        return pl.ds(pl.multiple_of(part * LANES, LANES), LANES)

    row = lax.broadcasted_iota(jnp.int32, (POOL, LANES), 0)

    def pools(part, _):
        lanes = lanes_of(part)
        for block in range(ROWS):
            twice, _, _ = gelu_twice(pre_act(block, lanes))
            if block == 0:
                twice = jnp.where(row >= 2, twice, 0.0)
            if block == ROWS - 1:
                twice = jnp.where(row < POOL - 2, twice, 0.0)
            pooled_sum[block : block + 1, lanes] = jnp.sum(twice, axis=0, keepdims=True)
        return 0

    def slope_part(part, _):
        lanes = lanes_of(part)
        for block in range(ROWS):
            x = pre_act(block, lanes)
            _, square, tanh = gelu_twice(x)
            slope = gelu_slope_twice(x, square, tanh)
            slope_rows[block * POOL : (block + 1) * POOL, lanes] = slope.astype(BF16)
        return 0

    lane = lax.broadcasted_iota(jnp.int32, (ROWS, WIDE), 1)
    grad = grad_ref[0].astype(F32)
    for h in range(DEPTH):
        low = 64 * (h % 2)
        start = window_start(h)
        keep = jnp.logical_and(lane >= low, lane < low + HEAD)
        window = jnp.where(keep, grad[:, start : start + WIDE], 0.0)
        if h % 2 == 0:
            window = pltpu.roll(window, 64, 1)
        grad_send[h] = jnp.concatenate([window[:, :128], window[:, 128:]], axis=0).astype(BF16)

    ends[1, 0] = jnp.concatenate([codes[:, :128], codes[:, SPAN - 128 :]], axis=1)
    lax.fori_loop(0, 1, pools, 0)
    pl.semaphore_wait(barrier, len(first_met))

    end_sends = [
        remote(
            ends.at[1, 0], ends.at[1 - side, step],
            end_ss.at[4 * (1 - side) + step], end_rs.at[4 * (1 - side) + step], beside(side, step),
        )
        for side, step in ((1, 2), (-1, 2), (1, 3), (-1, 3), (1, 1), (-1, 1), (1, 0), (-1, 0), (0, 2), (0, 1), (0, 3))
    ]
    for copy in end_sends:
        copy.start()
    g1 = [
        remote(
            grad_send.at[lax.bitwise_and(head + step, DEPTH - 1)], grad_rows.at[step],
            g1_ss.at[step], g1_rs.at[step], along_z(step),
        )
        for step in range(1, DEPTH)
    ]
    for copy in g1:
        copy.start()
    grad_rows[0] = grad_send[head]
    tell(0, (other_core, other_y, other_half, *column))

    lax.fori_loop(1, C // LANES, pools, 0)

    partial = pooled_sum[...] * (0.5 / POOL)
    rest = partial - partial.astype(BF16).astype(F32)
    spare = [jnp.zeros((2, 256), F32)]
    rests = [
        jnp.concatenate([rest[at : at + 1, 256 * i : 256 * i + 256] for i in range(6)] + spare, axis=0)
        for at in (0, ROWS - 1)
    ]
    pool_rows[0] = jnp.concatenate(
        [jnp.concatenate([partial[:, :INNER], partial[:, INNER:]], axis=0), jnp.concatenate(rests, axis=0)],
        axis=1,
    ).astype(BF16)
    p1 = [
        remote(pool_rows.at[0], pool_rows.at[step], p_ss.at[step], p_rs.at[step], along_z(step))
        for step in range(1, DEPTH)
    ]
    for copy in p1:
        copy.start()

    for copy in g1:
        copy.wait()
    blocks = grad_rows[...].astype(F32)
    grad_all[0] = jnp.concatenate(
        [jnp.concatenate([blocks[i, :8], blocks[i, 8:]], axis=1) for i in range(DEPTH)], axis=0
    ).astype(BF16)
    g2 = [
        remote(grad_all.at[0], grad_all.at[step], g2_ss.at[step], g2_rs.at[step], along_x(step))
        for step in range(1, RING)
    ]
    for copy in g2:
        copy.start()

    def turn(part, _):
        rows = pl.ds(pl.multiple_of(part * 128, 128), 128)
        for i in range(3):
            turned[i, :, rows] = weights[i, rows, :].T
        return 0

    for load in loads:
        load.wait()
    lax.fori_loop(0, C // 128 // 2, turn, 0)

    for copy in end_sends:
        copy.wait()
    lane = lax.broadcasted_iota(jnp.int32, (8, 128), 1)
    line = jnp.full((8, 128), -1, jnp.int32)
    sides = []
    for i in range(DEPTH):
        level = lax.bitwise_and(head - i + DEPTH, DEPTH - 1)
        before = jnp.where(level == 0, -1, ends[0, (i + 1) % DEPTH, :, 128:])
        before = jnp.where(col == 0, before, ends[0, i, :, 128:])
        after = jnp.where(level == DEPTH - 1, -1, ends[2, (i + 3) % DEPTH, :, :128])
        after = jnp.where(col == RING - 1, after, ends[2, i, :, :128])
        sides.append((before, after))
        for at, move, source in (
            (0, 2, before), (2, 2, ends[1, i, :, :128]), (8, 12, ends[1, i, :, 128:]), (12, 12, after),
        ):
            moved = pltpu.roll(jnp.broadcast_to(source, (8, 128)), 16 * i + move, 1)
            line = jnp.where(lane >= 16 * i + at, moved, line)
    line = jnp.where(lane < 16 * DEPTH, line, -1)[:1]
    near_ends = one_hot_rows(jnp.concatenate([outside, line, outside], axis=1))
    near_ends = positions_first(near_ends)[: 16 * DEPTH].astype(BF16)
    twice, _, _ = gelu_twice(jnp.dot(near_ends, table[...], preferred_element_type=F32))
    twice = twice.reshape(2 * DEPTH, 8, C)
    place = lax.broadcasted_iota(jnp.int32, twice.shape, 1)
    twice = jnp.where(jnp.logical_or(place == 2, place == 3), twice, 0.0)
    end_parts = jnp.sum(twice, axis=1) * (0.5 / POOL)

    for copy in p1:
        copy.wait()
    pl.semaphore_wait(met_sem.at[0], 6)
    tell(1, (other_core, other_half))
    odd = bits(head, 0, 1)
    start = pl.multiple_of(384 * bits(head, 1, 1) + 128 * odd, 128)
    low = 64 * odd
    lane = lax.broadcasted_iota(jnp.int32, (4 * ROWS, WIDE), 1)
    keep = jnp.logical_and(lane >= low, lane < low + HEAD)
    place = lax.broadcasted_iota(jnp.int32, (ROWS, C), 0)
    column_rows = []
    for i in range(DEPTH):
        sent = pool_rows[i].astype(F32)
        wide = jnp.concatenate([sent[:8, :INNER], sent[8:, :INNER]], axis=1)
        firsts = jnp.concatenate([sent[j : j + 1, INNER:] for j in range(6)], axis=1)
        lasts = jnp.concatenate([sent[8 + j : 9 + j, INNER:] for j in range(6)], axis=1)
        firsts += end_parts[2 * i : 2 * i + 1]
        lasts += end_parts[2 * i + 1 : 2 * i + 2]
        wide += jnp.where(place == 0, firsts, jnp.where(place == ROWS - 1, lasts, 0.0))
        column_rows.append(wide)
    column_rows = jnp.concatenate(column_rows, axis=0).astype(BF16)
    pooled_ref[0] = column_rows[:ROWS]

    def projected(i):
        rows = jnp.dot(column_rows, weights[i, :, pl.ds(start, WIDE)], preferred_element_type=F32)
        return pltpu.roll(jnp.where(keep, rows, 0.0), 192 * odd, 1)

    def round_x(ref, ss, rs):
        copies = [
            remote(ref.at[0], ref.at[step], ss.at[step], rs.at[step], along_x(step))
            for step in (4, 3, 5, 2, 6, 1, 7)
        ]
        for copy in copies:
            copy.start()
        return copies

    key = projected(1)
    key_tail = key[:16, 128:] + pltpu.roll(key[16:, 128:], 64, 1)
    k_all[0] = jnp.concatenate([key[:, :128], key_tail], axis=0).astype(BF16)
    k1 = round_x(k_all, k_ss, k_rs)
    query, value = projected(0), pltpu.roll(projected(2), 64, 1)
    qv_all[0] = jnp.concatenate(
        [query[:, :128], query[:, 128:] + value[:, :128], value[:, 128:]], axis=1
    ).astype(BF16)
    q1 = round_x(qv_all, q_ss, q_rs) + k1
    before, after = sides[0]
    first = one_hot_rows(jnp.concatenate([before, codes[:, :256]], axis=1))
    last = one_hot_rows(jnp.concatenate([codes[:, SPAN - 256 :], after], axis=1))
    hot_t[:, :POOL] = first.astype(BF16)
    hot_t[:, SPAN - POOL :] = last.astype(BF16)
    hot[:POOL, :] = positions_first(first).astype(BF16)
    hot[SPAN - POOL :, :] = positions_first(last).astype(BF16)
    lax.fori_loop(0, C // LANES, slope_part, 0)
    for block in range(ROWS):
        rows = slice(block * POOL, (block + 1) * POOL)
        slopes[block] = jnp.dot(hot_t[:, rows], slope_rows[rows, :], preferred_element_type=F32)
    lax.fori_loop(C // 128 // 2, C // 128, turn, 0)
    for copy in g2:
        copy.wait()
    for copy in q1:
        copy.wait()

    everyone = RING * 32
    q = qv_all[:, :, :WIDE].reshape(everyone, WIDE)
    v = qv_all[:, :, 128:].reshape(everyone, WIDE)
    tails = k_all[:, 32:48, :].astype(F32)
    low_lanes = lax.broadcasted_iota(jnp.int32, tails.shape, 2) < 64
    first_tail = jnp.where(low_lanes, tails, 0.0)
    last_tail = jnp.where(low_lanes, pltpu.roll(tails, 64, 2), 0.0)
    key_tail = jnp.concatenate([first_tail, last_tail], axis=1).astype(BF16)
    k = jnp.concatenate([k_all[:, :32, :], key_tail], axis=2).reshape(everyone, WIDE)
    g = grad_all[...].reshape(everyone, WIDE)
    scale = HEAD ** (-0.5)

    def soft_parts(scores, d_soft, axis):
        scores = scores * scale
        shifted = jnp.exp(scores - jnp.max(scores, axis=axis, keepdims=True))
        soft = shifted / jnp.sum(shifted, axis=axis, keepdims=True)
        delta = jnp.sum(soft * d_soft, axis=axis, keepdims=True)
        return soft, delta

    def finish(soft, d_soft, delta):
        return soft.astype(BF16), (soft * (d_soft - delta) * scale).astype(BF16)

    scores_t = lax.dot_general(k, q, NT, preferred_element_type=F32)
    d_soft_t = lax.dot_general(v, g, NT, preferred_element_type=F32)
    scores_own = lax.dot_general(q[:32], k, NT, preferred_element_type=F32)
    d_soft_own = lax.dot_general(g[:32], v, NT, preferred_element_type=F32)
    soft_t, delta_t = soft_parts(scores_t, d_soft_t, 0)
    half_t, d_half_t = finish(soft_t[:32], d_soft_t[:32], delta_t)
    soft_own, delta_own = soft_parts(scores_own, d_soft_own, 1)
    half_own, d_half_own = finish(soft_own, d_soft_own, delta_own)
    results = (
        jnp.dot(half_own, v, preferred_element_type=F32),
        jnp.dot(d_half_own, k, preferred_element_type=F32),
        jnp.dot(d_half_t, q, preferred_element_type=F32),
        jnp.dot(half_t, g, preferred_element_type=F32),
    )
    low_side, high_side = 64 * odd, 192 * (1 - odd)
    results = (
        pltpu.roll(jnp.where(lane >= 64, results[0], 0.0), high_side, 1),
        pltpu.roll(results[1], low_side, 1),
        pltpu.roll(jnp.where(lane < HEAD, results[2], 0.0), low_side, 1),
        pltpu.roll(results[3], high_side, 1),
    )
    for i in range(DEPTH):
        mine = jnp.concatenate([result[8 * i : 8 * i + 8] for result in results], axis=0).astype(BF16)
        if i == 0:
            back_rows[0] = mine
        else:
            back_send[i] = mine
    b1 = [
        remote(back_send.at[i], back_rows.at[i], b_ss.at[i], b_rs.at[i], along_z(-i))
        for i in range(1, DEPTH)
    ]
    for copy in b1:
        copy.start()
    for copy in b1:
        copy.wait()

    by_head = [back_rows[lax.bitwise_and(h - head + DEPTH, DEPTH - 1)].astype(F32) for h in range(DEPTH)]

    def joined(i):
        a, b, c, d = (rows[8 * i : 8 * i + 8] for rows in by_head)
        return jnp.concatenate(
            [a[:, :128], a[:, 128:] + b[:, :128], b[:, 128:], c[:, :128], c[:, 128:] + d[:, :128], d[:, 128:]],
            axis=1,
        ).astype(BF16)

    attended_ref[0] = joined(0)
    d_pooled = jnp.dot(joined(1), turned[0], preferred_element_type=F32)
    d_pooled += jnp.dot(joined(2), turned[1], preferred_element_type=F32)
    d_pooled += jnp.dot(joined(3), turned[2], preferred_element_type=F32)
    d_pooled *= 0.5 / POOL
    total = slopes[0, 0:40, :] * d_pooled[0:1]
    for block in range(1, ROWS):
        total += slopes[block, 0:40, :] * d_pooled[block : block + 1]
    for tap in range(5):
        for part in range(6):
            rows, at = slice(8 * tap, 8 * tap + 8), 256 * part
            chunk = [total[rows, at : at + 128], total[rows, at + 128 : at + 256]]
            chunks[6 * tap + part] = jnp.concatenate(chunk, axis=0).astype(BF16)
    chunks[30:32] = jnp.zeros((2, 16, 128), BF16)

    def outward(turn, centre):
        side = bits(turn, 0, 1)
        return lax.bitwise_and(centre + (1 - 2 * side) * bits(turn + 1, 1, 5), 31)

    def scatter(turn, _):
        step = outward(turn, 16)
        to, device = along_near(step)
        remote(chunks.at[to], near_rows.at[step], s_ss.at[0], s_rs.at[0], device).start()
        return 0

    def spread(turn, _):
        step = outward(turn, 20)
        remote(far_rows.at[0], far_rows.at[step], s_ss.at[1], s_rs.at[1], along_far(step)).start()
        return 0

    def gather(turn, _):
        mine = full.at[near]
        remote(mine, mine, s_ss.at[2], s_rs.at[2], along_near(outward(turn, 16))[1]).start()
        return 0

    def wait_all(ref, at):
        remote(ref, ref, s_ss.at[at], s_rs.at[at], along_z(1)).wait()

    pl.semaphore_wait(met_sem.at[1], 2)
    lax.fori_loop(0, NEAR - 1, scatter, 0)
    wait_all(near_rows.at[1:NEAR], 0)
    near_sum = chunks[near].astype(F32) + jnp.sum(near_rows[1:NEAR].astype(F32), axis=0)
    far_rows[0] = near_sum.astype(BF16)
    lax.fori_loop(0, 24, spread, 0)
    lax.fori_loop(25, FAR, spread, 0)
    wait_all(far_rows.at[1:FAR], 1)
    far_sum = far_rows[far].astype(F32)
    for i in range(1, FAR):
        far_sum += far_rows[lax.bitwise_and(far + (FAR - i), FAR - 1)].astype(F32)
    full[near] = far_sum.astype(BF16)
    lax.fori_loop(0, NEAR - 1, gather, 0)
    wait_all(full.at[0 : NEAR - 1], 2)
    for tap in range(5):
        for part in range(6):
            chunk = full[6 * tap + part].astype(F32)
            for side in range(2):
                lanes = slice(256 * part + 128 * side, 256 * part + 128 * side + 128)
                conv_ref[tap, :, lanes] = chunk[8 * side : 8 * side + LETTERS]
                if tap == 0:
                    conv_bias_ref[lanes] = chunk[8 * side + LETTERS]


def write_kernel(*refs):
    count = len(refs) // 2
    sems = refs[-1]
    copies = [pltpu.make_async_copy(refs[i], refs[count + i], sems.at[i]) for i in range(count)]
    for copy in copies:
        copy.start()
    for copy in copies:
        copy.wait()


def per_device(dna_bases, conv_weight, conv_bias, w_query, w_key, w_value, out_grad):
    vmem = pl.BlockSpec(memory_space=pltpu.VMEM)
    hbm = pl.BlockSpec(memory_space=pltpu.HBM)
    dma = pltpu.SemaphoreType.DMA
    results = pl.pallas_call(
        stem_kernel,
        name="genomic_stem",
        out_shape=(
            jax.ShapeDtypeStruct((1, ROWS, INNER), BF16),
            jax.ShapeDtypeStruct((1, ROWS, C), BF16),
            jax.ShapeDtypeStruct((5, LETTERS, C), F32),
            jax.ShapeDtypeStruct((C,), F32),
        ),
        in_specs=[hbm] * 7,
        out_specs=(vmem, vmem, vmem, vmem),
        scratch_shapes=[
            pltpu.VMEM((1, SPAN), jnp.int32),
            pltpu.VMEM((5, LETTERS, C), BF16),
            pltpu.VMEM((C,), F32),
            pltpu.VMEM((1, ROWS, INNER), BF16),
            pltpu.VMEM((3, C, INNER), BF16),
            pltpu.VMEM((3, INNER, C), BF16),
            pltpu.VMEM((128, C), BF16),
            pltpu.VMEM((SPAN, 128), BF16),
            pltpu.VMEM((CODES, SPAN), BF16),
            pltpu.VMEM((ROWS, C), F32),
            pltpu.VMEM((SPAN, C), BF16),
            pltpu.VMEM((ROWS, CODES, C), F32),
            pltpu.VMEM((3, DEPTH, 1, 256), jnp.int32),
            pltpu.VMEM((DEPTH, 16, 128), BF16),
            pltpu.VMEM((DEPTH, 16, 128), BF16),
            pltpu.VMEM((RING, 32, WIDE), BF16),
            pltpu.VMEM((DEPTH, 16, INNER + 256), BF16),
            pltpu.VMEM((RING, 48, 128), BF16),
            pltpu.VMEM((RING, 32, 384), BF16),
            pltpu.VMEM((DEPTH, 32, WIDE), BF16),
            pltpu.VMEM((DEPTH, 32, WIDE), BF16),
            pltpu.VMEM((40, C), F32),
            pltpu.VMEM((NEAR, 16, 128), BF16),
            pltpu.VMEM((NEAR, 16, 128), BF16),
            pltpu.VMEM((FAR, 16, 128), BF16),
            pltpu.VMEM((NEAR, 16, 128), BF16),
            pltpu.SemaphoreType.REGULAR((2,)),
            dma((7,)), dma((12,)), dma((12,)),
            dma((DEPTH,)), dma((DEPTH,)), dma((RING,)), dma((RING,)), dma((DEPTH,)), dma((DEPTH,)),
            dma((RING,)), dma((RING,)), dma((RING,)), dma((RING,)), dma((DEPTH,)), dma((DEPTH,)),
            dma((3,)), dma((3,)),
        ],
        compiler_params=pltpu.CompilerParams(
            collective_id=0, has_side_effects=True, vmem_limit_bytes=48 * 2**20
        ),
        cost_estimate=pl.CostEstimate(
            flops=2_000_000_000, bytes_accessed=8_000_000, transcendentals=4_000_000
        ),
    )(
        *(pltpu.with_memory_space_constraint(a, pltpu.HBM) for a in (
        dna_bases, conv_weight, conv_bias, w_query, w_key, w_value, out_grad))
    )
    return pl.pallas_call(
        write_kernel,
        name="write_results",
        out_shape=tuple(jax.ShapeDtypeStruct(a.shape, a.dtype) for a in results),
        in_specs=[vmem] * 4,
        out_specs=(hbm,) * 4,
        scratch_shapes=[dma((4,))],
        compiler_params=pltpu.CompilerParams(vmem_limit_bytes=2**20),
    )(*results)


def solution(mesh):
    in_specs = (P("dp", "seq"), P(), P(), P(), P(), P(), P("dp", "seq", None))
    out_specs = (P("dp", "seq", None), P("dp", "seq", None), P(), P())
    return jax.shard_map(
        per_device, mesh=mesh, in_specs=in_specs, out_specs=out_specs, check_vma=False
    )
```

```python
import functools

import jax
import jax.numpy as jnp
from jax import lax
from jax.experimental import pallas as pl
from jax.experimental.pallas import tpu as pltpu
from jax.sharding import PartitionSpec as P

C = 1536
HEAD = 192
LETTERS = 5
POOL = 128
INNER = 768
ROWS = 8
SPAN = ROWS * POOL
CODES = 48
WIDE = 256
LANES = 512
DEPTH = 4
RING = 8
SEQ = DEPTH * RING
NEAR = 32
FAR = 32
GELU_A = 0.7978845608028654
GELU_B = 0.044715
NT = (((1,), (1,)), ((), ()))
MESH = pl.DeviceIdType.MESH
F32 = jnp.float32
BF16 = jnp.bfloat16


def bits(value, low, count):
    return lax.bitwise_and(lax.shift_right_logical(value, low), (1 << count) - 1)


def window_start(head):
    return 384 * (head // 2) + 128 * (head % 2)


def one_hot_rows(codes):
    width = codes.shape[1]
    wide = jnp.broadcast_to(codes, (8, width))
    letter = lax.broadcasted_iota(jnp.int32, (8, width - 256), 0)
    parts = []
    for tap in range(5):
        moved = wide if tap == 2 else pltpu.roll(wide, (2 - tap) % width, 1)
        hit = moved[:, 128 : width - 128] == letter
        if tap == 0:
            hit = jnp.logical_or(hit, letter >= LETTERS)
        parts.append(jnp.where(hit, 1.0, 0.0).astype(F32))
    parts.append(jnp.zeros_like(parts[0]))
    return jnp.concatenate(parts, axis=0)


def positions_first(rows):
    full = jnp.concatenate([rows, jnp.zeros((128 - CODES, rows.shape[1]), F32)], axis=0)
    blocks = [full[:, at : at + 128].T for at in range(0, rows.shape[1], 128)]
    return jnp.concatenate(blocks, axis=0)


def gelu_twice(x):
    square = x * x
    inner = x * (square * (GELU_A * GELU_B) + GELU_A)
    tanh = jnp.tanh(inner)
    return x + x * tanh, square, tanh


def gelu_slope_twice(x, square, tanh):
    return (1.0 + tanh) + (x - x * (tanh * tanh)) * (square * (3 * GELU_A * GELU_B) + GELU_A)


def stem_kernel(
    dna_hbm, taps_hbm, bias_hbm, wq_hbm, wk_hbm, wv_hbm, grad_hbm,
    attended_ref, pooled_ref, conv_ref, conv_bias_ref,
    dna_ref, taps_ref, bias_ref, grad_ref, weights, turned, table, hot, hot_t, pooled_sum, slope_rows, slopes, ends,
    grad_send, grad_rows, grad_all, pool_rows, k_all, qv_all, back_send, back_rows,
    acc, chunks, near_rows, far_rows, full,
    met_sem, load_sem, end_ss, end_rs, g1_ss, g1_rs, g2_ss, g2_rs, p_ss, p_rs, k_ss, k_rs, q_ss, q_rs, b_ss, b_rs,
    s_ss, s_rs,
):
    dp = lax.axis_index("dp")
    seq = lax.axis_index("seq")
    head, col = bits(seq, 3, 2), bits(seq, 0, 3)
    near = col * 4 + bits(dp, 0, 2)
    far = bits(dp, 2, 2) * 8 + bits(dp, 4, 1) * 4 + head

    def along_z(step):
        return (dp, lax.bitwise_and(seq + (step * RING + SEQ), SEQ - 1))

    def along_x(step):
        return (dp, head * RING + lax.bitwise_and(col + step, RING - 1))

    def beside(side, step):
        return (
            dp,
            lax.bitwise_and(head + step, DEPTH - 1) * RING + lax.bitwise_and(col + (side + RING), RING - 1),
        )

    def device_at(near, far):
        return (
            bits(far, 2, 1) * 16 + bits(far, 3, 2) * 4 + bits(near, 0, 2),
            bits(far, 0, 2) * RING + bits(near, 2, 3),
        )

    def along_near(step):
        to = lax.bitwise_and(near + step, NEAR - 1)
        return to, device_at(to, far)

    def along_far(step):
        return device_at(near, lax.bitwise_and(far + step, FAR - 1))

    def remote(src, dst, ss, rs, device):
        return pltpu.make_async_remote_copy(
            src_ref=src, dst_ref=dst, send_sem=ss, recv_sem=rs, device_id=device, device_id_type=MESH
        )

    other_core = (dp + 1 - 2 * bits(dp, 0, 1), seq)
    other_y = (dp + 2 - 4 * bits(dp, 1, 1), seq)
    other_half = (dp + 16 - 32 * bits(dp, 4, 1), seq)
    quad = bits(dp, 2, 2)
    pairs_y = [(dp + 4 * (lax.bitwise_and(quad + step, 3) - quad), seq) for step in (1, 2, 3)]
    column = [along_z(step) for step in range(1, DEPTH)]
    first_met = [
        *(beside(side, step) for side in (1, -1) for step in (2, 1, 3)), *column, *(along_x(step) for step in (4, 3, 5, 2, 6, 1, 7)),
        other_half, *pairs_y, other_y, other_core,
    ]
    barrier = pltpu.get_barrier_semaphore()
    for device in first_met:
        pl.semaphore_signal(barrier, inc=1, device_id=device, device_id_type=MESH)

    def tell(at, devices):
        for device in devices:
            pl.semaphore_signal(met_sem.at[at], inc=1, device_id=device, device_id_type=MESH)

    small = ((dna_hbm, dna_ref), (taps_hbm, taps_ref), (bias_hbm, bias_ref), (grad_hbm, grad_ref))
    reads = [pltpu.make_async_copy(hbm, ref, load_sem.at[3 + i]) for i, (hbm, ref) in enumerate(small)]
    loads = [
        pltpu.make_async_copy(hbm, weights.at[i], load_sem.at[i])
        for i, hbm in enumerate((wq_hbm, wk_hbm, wv_hbm))
    ]
    for copy in (*reads, *loads):
        copy.start()

    for copy in reads:
        copy.wait()

    bias = bias_ref[...].reshape(1, C)
    bias_high = bias.astype(BF16).astype(F32)
    bias_mid = (bias - bias_high).astype(BF16).astype(F32)
    bias_low = bias - bias_high - bias_mid
    for tap in range(5):
        letters = taps_ref[tap].astype(F32)
        spare = [bias_high, bias_mid, bias_low] if tap == 0 else [jnp.zeros((3, C), F32)]
        pair = jnp.concatenate([letters, *spare], axis=0)
        acc[8 * tap : 8 * tap + 8, :] = pair
    table[0:48, :] = jnp.concatenate([acc[...], jnp.zeros((8, C), F32)], axis=0).astype(BF16)
    table[48:128, :] = jnp.zeros((80, C), BF16)

    codes = dna_ref[...]
    outside = jnp.full((1, 128), -1, jnp.int32)
    rows = one_hot_rows(jnp.concatenate([outside, codes, outside], axis=1))
    hot_t[...] = rows.astype(BF16)
    hot[...] = positions_first(rows).astype(BF16)

    def pre_act(block, lanes):
        return jnp.dot(
            hot[block * POOL : (block + 1) * POOL, :], table[:, lanes], preferred_element_type=F32
        )

    def lanes_of(part):
        return pl.ds(pl.multiple_of(part * LANES, LANES), LANES)

    row = lax.broadcasted_iota(jnp.int32, (POOL, LANES), 0)

    def pools(part, _):
        lanes = lanes_of(part)
        for block in range(ROWS):
            twice, _, _ = gelu_twice(pre_act(block, lanes))
            if block == 0:
                twice = jnp.where(row >= 2, twice, 0.0)
            if block == ROWS - 1:
                twice = jnp.where(row < POOL - 2, twice, 0.0)
            pooled_sum[block : block + 1, lanes] = jnp.sum(twice, axis=0, keepdims=True)
        return 0

    def slope_part(part, _):
        lanes = lanes_of(part)
        for block in range(ROWS):
            x = pre_act(block, lanes)
            _, square, tanh = gelu_twice(x)
            slope = gelu_slope_twice(x, square, tanh)
            slope_rows[block * POOL : (block + 1) * POOL, lanes] = slope.astype(BF16)
        return 0

    lane = lax.broadcasted_iota(jnp.int32, (ROWS, WIDE), 1)
    grad = grad_ref[0].astype(F32)
    for h in range(DEPTH):
        low = 64 * (h % 2)
        start = window_start(h)
        keep = jnp.logical_and(lane >= low, lane < low + HEAD)
        window = jnp.where(keep, grad[:, start : start + WIDE], 0.0)
        if h % 2 == 0:
            window = pltpu.roll(window, 64, 1)
        grad_send[h] = jnp.concatenate([window[:, :128], window[:, 128:]], axis=0).astype(BF16)

    ends[1, 0] = jnp.concatenate([codes[:, :128], codes[:, SPAN - 128 :]], axis=1)
    lax.fori_loop(0, 1, pools, 0)
    pl.semaphore_wait(barrier, len(first_met))

    end_sends = [
        remote(
            ends.at[1, 0], ends.at[1 - side, step],
            end_ss.at[4 * (1 - side) + step], end_rs.at[4 * (1 - side) + step], beside(side, step),
        )
        for side, step in ((1, 2), (-1, 2), (1, 3), (-1, 3), (1, 1), (-1, 1), (1, 0), (-1, 0), (0, 2), (0, 1), (0, 3))
    ]
    for copy in end_sends:
        copy.start()
    g1 = [
        remote(
            grad_send.at[lax.bitwise_and(head + step, DEPTH - 1)], grad_rows.at[step],
            g1_ss.at[step], g1_rs.at[step], along_z(step),
        )
        for step in range(1, DEPTH)
    ]
    for copy in g1:
        copy.start()
    grad_rows[0] = grad_send[head]
    tell(0, (other_core, other_y, other_half, *column))

    lax.fori_loop(1, C // LANES, pools, 0)

    partial = pooled_sum[...] * (0.5 / POOL)
    rest = partial - partial.astype(BF16).astype(F32)
    spare = [jnp.zeros((2, 256), F32)]
    rests = [
        jnp.concatenate([rest[at : at + 1, 256 * i : 256 * i + 256] for i in range(6)] + spare, axis=0)
        for at in (0, ROWS - 1)
    ]
    pool_rows[0] = jnp.concatenate(
        [jnp.concatenate([partial[:, :INNER], partial[:, INNER:]], axis=0), jnp.concatenate(rests, axis=0)],
        axis=1,
    ).astype(BF16)
    p1 = [
        remote(pool_rows.at[0], pool_rows.at[step], p_ss.at[step], p_rs.at[step], along_z(step))
        for step in range(1, DEPTH)
    ]
    for copy in p1:
        copy.start()

    for copy in g1:
        copy.wait()
    blocks = grad_rows[...].astype(F32)
    grad_all[0] = jnp.concatenate(
        [jnp.concatenate([blocks[i, :8], blocks[i, 8:]], axis=1) for i in range(DEPTH)], axis=0
    ).astype(BF16)
    g2 = [
        remote(grad_all.at[0], grad_all.at[step], g2_ss.at[step], g2_rs.at[step], along_x(step))
        for step in range(1, RING)
    ]
    for copy in g2:
        copy.start()

    def turn(part, _):
        rows = pl.ds(pl.multiple_of(part * 128, 128), 128)
        for i in range(3):
            turned[i, :, rows] = weights[i, rows, :].T
        return 0

    for load in loads:
        load.wait()
    lax.fori_loop(0, C // 128 // 2, turn, 0)

    for copy in end_sends:
        copy.wait()
    lane = lax.broadcasted_iota(jnp.int32, (8, 128), 1)
    line = jnp.full((8, 128), -1, jnp.int32)
    sides = []
    for i in range(DEPTH):
        level = lax.bitwise_and(head - i + DEPTH, DEPTH - 1)
        before = jnp.where(level == 0, -1, ends[0, (i + 1) % DEPTH, :, 128:])
        before = jnp.where(col == 0, before, ends[0, i, :, 128:])
        after = jnp.where(level == DEPTH - 1, -1, ends[2, (i + 3) % DEPTH, :, :128])
        after = jnp.where(col == RING - 1, after, ends[2, i, :, :128])
        sides.append((before, after))
        for at, move, source in (
            (0, 2, before), (2, 2, ends[1, i, :, :128]), (8, 12, ends[1, i, :, 128:]), (12, 12, after),
        ):
            moved = pltpu.roll(jnp.broadcast_to(source, (8, 128)), 16 * i + move, 1)
            line = jnp.where(lane >= 16 * i + at, moved, line)
    line = jnp.where(lane < 16 * DEPTH, line, -1)[:1]
    near_ends = one_hot_rows(jnp.concatenate([outside, line, outside], axis=1))
    near_ends = positions_first(near_ends)[: 16 * DEPTH].astype(BF16)
    twice, _, _ = gelu_twice(jnp.dot(near_ends, table[...], preferred_element_type=F32))
    twice = twice.reshape(2 * DEPTH, 8, C)
    place = lax.broadcasted_iota(jnp.int32, twice.shape, 1)
    twice = jnp.where(jnp.logical_or(place == 2, place == 3), twice, 0.0)
    end_parts = jnp.sum(twice, axis=1) * (0.5 / POOL)

    for copy in p1:
        copy.wait()
    pl.semaphore_wait(met_sem.at[0], 6)
    tell(1, (other_core, other_half))
    odd = bits(head, 0, 1)
    start = pl.multiple_of(384 * bits(head, 1, 1) + 128 * odd, 128)
    low = 64 * odd
    lane = lax.broadcasted_iota(jnp.int32, (4 * ROWS, WIDE), 1)
    keep = jnp.logical_and(lane >= low, lane < low + HEAD)
    place = lax.broadcasted_iota(jnp.int32, (ROWS, C), 0)
    column_rows = []
    for i in range(DEPTH):
        sent = pool_rows[i].astype(F32)
        wide = jnp.concatenate([sent[:8, :INNER], sent[8:, :INNER]], axis=1)
        firsts = jnp.concatenate([sent[j : j + 1, INNER:] for j in range(6)], axis=1)
        lasts = jnp.concatenate([sent[8 + j : 9 + j, INNER:] for j in range(6)], axis=1)
        firsts += end_parts[2 * i : 2 * i + 1]
        lasts += end_parts[2 * i + 1 : 2 * i + 2]
        wide += jnp.where(place == 0, firsts, jnp.where(place == ROWS - 1, lasts, 0.0))
        column_rows.append(wide)
    column_rows = jnp.concatenate(column_rows, axis=0).astype(BF16)
    pooled_ref[0] = column_rows[:ROWS]

    def projected(i):
        rows = jnp.dot(column_rows, weights[i, :, pl.ds(start, WIDE)], preferred_element_type=F32)
        return pltpu.roll(jnp.where(keep, rows, 0.0), 192 * odd, 1)

    def round_x(ref, ss, rs):
        copies = [
            remote(ref.at[0], ref.at[step], ss.at[step], rs.at[step], along_x(step))
            for step in (4, 3, 5, 2, 6, 1, 7)
        ]
        for copy in copies:
            copy.start()
        return copies

    key = projected(1)
    key_tail = key[:16, 128:] + pltpu.roll(key[16:, 128:], 64, 1)
    k_all[0] = jnp.concatenate([key[:, :128], key_tail], axis=0).astype(BF16)
    k1 = round_x(k_all, k_ss, k_rs)
    query, value = projected(0), pltpu.roll(projected(2), 64, 1)
    qv_all[0] = jnp.concatenate(
        [query[:, :128], query[:, 128:] + value[:, :128], value[:, 128:]], axis=1
    ).astype(BF16)
    q1 = round_x(qv_all, q_ss, q_rs) + k1
    before, after = sides[0]
    first = one_hot_rows(jnp.concatenate([before, codes[:, :256]], axis=1))
    last = one_hot_rows(jnp.concatenate([codes[:, SPAN - 256 :], after], axis=1))
    hot_t[:, :POOL] = first.astype(BF16)
    hot_t[:, SPAN - POOL :] = last.astype(BF16)
    hot[:POOL, :] = positions_first(first).astype(BF16)
    hot[SPAN - POOL :, :] = positions_first(last).astype(BF16)
    lax.fori_loop(0, C // LANES, slope_part, 0)
    for block in range(ROWS):
        rows = slice(block * POOL, (block + 1) * POOL)
        slopes[block] = jnp.dot(hot_t[:, rows], slope_rows[rows, :], preferred_element_type=F32)
    lax.fori_loop(C // 128 // 2, C // 128, turn, 0)
    for copy in g2:
        copy.wait()
    for copy in q1:
        copy.wait()

    everyone = RING * 32
    q = qv_all[:, :, :WIDE].reshape(everyone, WIDE)
    v = qv_all[:, :, 128:].reshape(everyone, WIDE)
    tails = k_all[:, 32:48, :].astype(F32)
    low_lanes = lax.broadcasted_iota(jnp.int32, tails.shape, 2) < 64
    first_tail = jnp.where(low_lanes, tails, 0.0)
    last_tail = jnp.where(low_lanes, pltpu.roll(tails, 64, 2), 0.0)
    key_tail = jnp.concatenate([first_tail, last_tail], axis=1).astype(BF16)
    k = jnp.concatenate([k_all[:, :32, :], key_tail], axis=2).reshape(everyone, WIDE)
    g = grad_all[...].reshape(everyone, WIDE)
    scale = HEAD ** (-0.5)

    def soft_parts(scores, d_soft, axis):
        scores = scores * scale
        shifted = jnp.exp(scores - jnp.max(scores, axis=axis, keepdims=True))
        soft = shifted / jnp.sum(shifted, axis=axis, keepdims=True)
        delta = jnp.sum(soft * d_soft, axis=axis, keepdims=True)
        return soft, delta

    def finish(soft, d_soft, delta):
        return soft.astype(BF16), (soft * (d_soft - delta) * scale).astype(BF16)

    scores_t = lax.dot_general(k, q, NT, preferred_element_type=F32)
    d_soft_t = lax.dot_general(v, g, NT, preferred_element_type=F32)
    scores_own = lax.dot_general(q[:32], k, NT, preferred_element_type=F32)
    d_soft_own = lax.dot_general(g[:32], v, NT, preferred_element_type=F32)
    soft_t, delta_t = soft_parts(scores_t, d_soft_t, 0)
    half_t, d_half_t = finish(soft_t[:32], d_soft_t[:32], delta_t)
    soft_own, delta_own = soft_parts(scores_own, d_soft_own, 1)
    half_own, d_half_own = finish(soft_own, d_soft_own, delta_own)
    results = (
        jnp.dot(half_own, v, preferred_element_type=F32),
        jnp.dot(d_half_own, k, preferred_element_type=F32),
        jnp.dot(d_half_t, q, preferred_element_type=F32),
        jnp.dot(half_t, g, preferred_element_type=F32),
    )
    low_side, high_side = 64 * odd, 192 * (1 - odd)
    results = (
        pltpu.roll(jnp.where(lane >= 64, results[0], 0.0), high_side, 1),
        pltpu.roll(results[1], low_side, 1),
        pltpu.roll(jnp.where(lane < HEAD, results[2], 0.0), low_side, 1),
        pltpu.roll(results[3], high_side, 1),
    )
    for i in range(DEPTH):
        mine = jnp.concatenate([result[8 * i : 8 * i + 8] for result in results], axis=0).astype(BF16)
        if i == 0:
            back_rows[0] = mine
        else:
            back_send[i] = mine
    b1 = [
        remote(back_send.at[i], back_rows.at[i], b_ss.at[i], b_rs.at[i], along_z(-i))
        for i in range(1, DEPTH)
    ]
    for copy in b1:
        copy.start()
    for copy in b1:
        copy.wait()

    by_head = [back_rows[lax.bitwise_and(h - head + DEPTH, DEPTH - 1)].astype(F32) for h in range(DEPTH)]

    def joined(i):
        a, b, c, d = (rows[8 * i : 8 * i + 8] for rows in by_head)
        return jnp.concatenate(
            [a[:, :128], a[:, 128:] + b[:, :128], b[:, 128:], c[:, :128], c[:, 128:] + d[:, :128], d[:, 128:]],
            axis=1,
        ).astype(BF16)

    attended_ref[0] = joined(0)
    d_rows = jnp.concatenate([joined(1), joined(2), joined(3)], axis=1)
    d_pooled = jnp.dot(d_rows, turned[...].reshape(3 * INNER, C), preferred_element_type=F32)
    d_pooled *= 0.5 / POOL
    total = slopes[0, 0:40, :] * d_pooled[0:1]
    for block in range(1, ROWS):
        total += slopes[block, 0:40, :] * d_pooled[block : block + 1]
    for tap in range(5):
        for part in range(6):
            rows, at = slice(8 * tap, 8 * tap + 8), 256 * part
            chunk = [total[rows, at : at + 128], total[rows, at + 128 : at + 256]]
            chunks[6 * tap + part] = jnp.concatenate(chunk, axis=0).astype(BF16)
    chunks[30:32] = jnp.zeros((2, 16, 128), BF16)

    def outward(turn, centre):
        side = bits(turn, 0, 1)
        return lax.bitwise_and(centre + (1 - 2 * side) * bits(turn + 1, 1, 5), 31)

    def scatter(turn, _):
        step = outward(turn, 16)
        to, device = along_near(step)
        remote(chunks.at[to], near_rows.at[step], s_ss.at[0], s_rs.at[0], device).start()
        return 0

    def spread(turn, _):
        step = outward(turn, 20)
        remote(far_rows.at[0], far_rows.at[step], s_ss.at[1], s_rs.at[1], along_far(step)).start()
        return 0

    def gather(turn, _):
        mine = full.at[near]
        remote(mine, mine, s_ss.at[2], s_rs.at[2], along_near(outward(turn, 16))[1]).start()
        return 0

    def wait_all(ref, at):
        remote(ref, ref, s_ss.at[at], s_rs.at[at], along_z(1)).wait()

    pl.semaphore_wait(met_sem.at[1], 2)
    lax.fori_loop(0, NEAR - 1, scatter, 0)
    wait_all(near_rows.at[1:NEAR], 0)
    near_sum = chunks[near].astype(F32) + jnp.sum(near_rows[1:NEAR].astype(F32), axis=0)
    far_rows[0] = near_sum.astype(BF16)
    lax.fori_loop(0, 24, spread, 0)
    lax.fori_loop(25, FAR, spread, 0)
    wait_all(far_rows.at[1:FAR], 1)
    far_sum = far_rows[far].astype(F32)
    for i in range(1, FAR):
        far_sum += far_rows[lax.bitwise_and(far + (FAR - i), FAR - 1)].astype(F32)
    full[near] = far_sum.astype(BF16)
    lax.fori_loop(0, NEAR - 1, gather, 0)
    wait_all(full.at[0 : NEAR - 1], 2)
    for tap in range(5):
        for part in range(6):
            chunk = full[6 * tap + part].astype(F32)
            for side in range(2):
                lanes = slice(256 * part + 128 * side, 256 * part + 128 * side + 128)
                conv_ref[tap, :, lanes] = chunk[8 * side : 8 * side + LETTERS]
                if tap == 0:
                    conv_bias_ref[lanes] = chunk[8 * side + LETTERS]


def write_kernel(*refs):
    count = len(refs) // 2
    sems = refs[-1]
    copies = [pltpu.make_async_copy(refs[i], refs[count + i], sems.at[i]) for i in range(count)]
    for copy in copies:
        copy.start()
    for copy in copies:
        copy.wait()


def per_device(dna_bases, conv_weight, conv_bias, w_query, w_key, w_value, out_grad):
    vmem = pl.BlockSpec(memory_space=pltpu.VMEM)
    hbm = pl.BlockSpec(memory_space=pltpu.HBM)
    dma = pltpu.SemaphoreType.DMA
    results = pl.pallas_call(
        stem_kernel,
        name="genomic_stem",
        out_shape=(
            jax.ShapeDtypeStruct((1, ROWS, INNER), BF16),
            jax.ShapeDtypeStruct((1, ROWS, C), BF16),
            jax.ShapeDtypeStruct((5, LETTERS, C), F32),
            jax.ShapeDtypeStruct((C,), F32),
        ),
        in_specs=[hbm] * 7,
        out_specs=(vmem, vmem, vmem, vmem),
        scratch_shapes=[
            pltpu.VMEM((1, SPAN), jnp.int32),
            pltpu.VMEM((5, LETTERS, C), BF16),
            pltpu.VMEM((C,), F32),
            pltpu.VMEM((1, ROWS, INNER), BF16),
            pltpu.VMEM((3, C, INNER), BF16),
            pltpu.VMEM((3, INNER, C), BF16),
            pltpu.VMEM((128, C), BF16),
            pltpu.VMEM((SPAN, 128), BF16),
            pltpu.VMEM((CODES, SPAN), BF16),
            pltpu.VMEM((ROWS, C), F32),
            pltpu.VMEM((SPAN, C), BF16),
            pltpu.VMEM((ROWS, CODES, C), F32),
            pltpu.VMEM((3, DEPTH, 1, 256), jnp.int32),
            pltpu.VMEM((DEPTH, 16, 128), BF16),
            pltpu.VMEM((DEPTH, 16, 128), BF16),
            pltpu.VMEM((RING, 32, WIDE), BF16),
            pltpu.VMEM((DEPTH, 16, INNER + 256), BF16),
            pltpu.VMEM((RING, 48, 128), BF16),
            pltpu.VMEM((RING, 32, 384), BF16),
            pltpu.VMEM((DEPTH, 32, WIDE), BF16),
            pltpu.VMEM((DEPTH, 32, WIDE), BF16),
            pltpu.VMEM((40, C), F32),
            pltpu.VMEM((NEAR, 16, 128), BF16),
            pltpu.VMEM((NEAR, 16, 128), BF16),
            pltpu.VMEM((FAR, 16, 128), BF16),
            pltpu.VMEM((NEAR, 16, 128), BF16),
            pltpu.SemaphoreType.REGULAR((2,)),
            dma((7,)), dma((12,)), dma((12,)),
            dma((DEPTH,)), dma((DEPTH,)), dma((RING,)), dma((RING,)), dma((DEPTH,)), dma((DEPTH,)),
            dma((RING,)), dma((RING,)), dma((RING,)), dma((RING,)), dma((DEPTH,)), dma((DEPTH,)),
            dma((3,)), dma((3,)),
        ],
        compiler_params=pltpu.CompilerParams(
            collective_id=0, has_side_effects=True, vmem_limit_bytes=48 * 2**20
        ),
        cost_estimate=pl.CostEstimate(
            flops=2_000_000_000, bytes_accessed=8_000_000, transcendentals=4_000_000
        ),
    )(
        *(pltpu.with_memory_space_constraint(a, pltpu.HBM) for a in (
        dna_bases, conv_weight, conv_bias, w_query, w_key, w_value, out_grad))
    )
    return pl.pallas_call(
        write_kernel,
        name="write_results",
        out_shape=tuple(jax.ShapeDtypeStruct(a.shape, a.dtype) for a in results),
        in_specs=[vmem] * 4,
        out_specs=(hbm,) * 4,
        scratch_shapes=[dma((4,))],
        compiler_params=pltpu.CompilerParams(vmem_limit_bytes=2**20),
    )(*results)


def solution(mesh):
    in_specs = (P("dp", "seq"), P(), P(), P(), P(), P(), P("dp", "seq", None))
    out_specs = (P("dp", "seq", None), P("dp", "seq", None), P(), P())
    return jax.shard_map(
        per_device, mesh=mesh, in_specs=in_specs, out_specs=out_specs, check_vma=False
    )
```
